32 devices in a mesh: dp: 8 (over y, x, core), fsdp: 4 (over z).
Axes of the slice: x: 2, y: 2, z: 4, core: 2. Of those that a mesh axis runs over, the one named last changes fastest.
Arguments:
- token_ids: int32 [32, 512], P(('dp', 'fsdp')), may hold values from 0 to 7999
- targets: int32 [32, 512], P(('dp', 'fsdp')), may hold values from 0 to 7999
- target_counts: int32 [32], P(('dp', 'fsdp')), may hold values from 1 to 512, as said below
- memory: bfloat16 [32, 512, 1024], P(('dp', 'fsdp')), may hold values from -8 to 8
- value_routes: int32 [32, 1024, 4, 2], P(('dp', 'fsdp')), may hold values from 0 to 4, as said below
- value_slots: int32 [32, 1024, 4, 2], P(('dp', 'fsdp')), may hold values from 0 to 512, as said below
- output_routes: int32 [32, 512, 4, 2], P(('dp', 'fsdp')), may hold values from 0 to 4, as said below
- output_slots: int32 [32, 512, 4, 2], P(('dp', 'fsdp')), may hold values from 0 to 256, as said below
- embedding: float32 [8000, 1024], P('fsdp', 'dp')
- momentum_embedding: float32 [8000, 1024], P('fsdp', 'dp'), may hold values from -2.670288e-05 to 2.670288e-05
- average_embedding: float32 [8000, 1024], P('fsdp', 'dp'), may hold values from -0.1875 to 0.1875
- projector: float32 [1024, 936], P(('dp', 'fsdp')), may hold values from -0.15625 to 0.15625
- momentum_projector: float32 [1024, 936], P(('dp', 'fsdp')), may hold values from -2.670288e-05 to 2.670288e-05
- average_projector: float32 [1024, 936], P(('dp', 'fsdp')), may hold values from -0.15625 to 0.15625
- position: float32 [1024, 448], P(('dp', 'fsdp')), may hold values from -0.25 to 0.25
- momentum_position: float32 [1024, 448], P(('dp', 'fsdp')), may hold values from -2.670288e-05 to 2.670288e-05
- average_position: float32 [1024, 448], P(('dp', 'fsdp')), may hold values from -0.25 to 0.25
- values: float32 [1024, 2240], P(('dp', 'fsdp')), may hold values from -0.1875 to 0.1875
- momentum_values: float32 [1024, 2240], P(('dp', 'fsdp')), may hold values from -2.670288e-05 to 2.670288e-05
- average_values: float32 [1024, 2240], P(('dp', 'fsdp')), may hold values from -0.1875 to 0.1875
- outputs: float32 [2240, 1024], P(None, ('dp', 'fsdp')), may hold values from -3 to 3
- momentum_outputs: float32 [2240, 1024], P(None, ('dp', 'fsdp')), may hold values from -7.1525574e-07 to 7.1525574e-07
- average_outputs: float32 [2240, 1024], P(None, ('dp', 'fsdp')), may hold values from -3 to 3
- expand: float32 [1024, 4096], P(('dp', 'fsdp')), may hold values from -0.1875 to 0.1875
- momentum_expand: float32 [1024, 4096], P(('dp', 'fsdp')), may hold values from -2.670288e-05 to 2.670288e-05
- average_expand: float32 [1024, 4096], P(('dp', 'fsdp')), may hold values from -0.1875 to 0.1875
- contract: float32 [4096, 1024], P(None, ('dp', 'fsdp')), may hold values from -0.125 to 0.125
- momentum_contract: float32 [4096, 1024], P(None, ('dp', 'fsdp')), may hold values from -2.670288e-05 to 2.670288e-05
- average_contract: float32 [4096, 1024], P(None, ('dp', 'fsdp')), may hold values from -0.125 to 0.125
- vectors: float32 [4, 1024], P(None, ('dp', 'fsdp'))
- momentum_vectors: float32 [4, 1024], P(None, ('dp', 'fsdp')), may hold values from -2.670288e-05 to 2.670288e-05
- average_vectors: float32 [4, 1024], P(None, ('dp', 'fsdp')), may hold values from 0.5 to 1.5
- biases: float32 [4992], replicated, may hold values from -3 to 3
- momentum_biases: float32 [4992], replicated, may hold values from -2.670288e-05 to 2.670288e-05
- average_biases: float32 [4992], replicated, may hold values from -3 to 3
Outputs:
- loss_total: float32 [], replicated
- token_count: float32 [], replicated
- gradient_norm: float32 [], replicated
- velocity_embedding: float32 [8000, 1024], P('fsdp', 'dp')
- updated_embedding: float32 [8000, 1024], P('fsdp', 'dp')
- smoothed_embedding: float32 [8000, 1024], P('fsdp', 'dp')
- velocity_projector: float32 [1024, 936], P(('dp', 'fsdp'))
- updated_projector: float32 [1024, 936], P(('dp', 'fsdp'))
- smoothed_projector: float32 [1024, 936], P(('dp', 'fsdp'))
- velocity_position: float32 [1024, 448], P(('dp', 'fsdp'))
- updated_position: float32 [1024, 448], P(('dp', 'fsdp'))
- smoothed_position: float32 [1024, 448], P(('dp', 'fsdp'))
- velocity_values: float32 [1024, 2240], P(('dp', 'fsdp'))
- updated_values: float32 [1024, 2240], P(('dp', 'fsdp'))
- smoothed_values: float32 [1024, 2240], P(('dp', 'fsdp'))
- velocity_outputs: float32 [2240, 1024], P(None, ('dp', 'fsdp'))
- updated_outputs: float32 [2240, 1024], P(None, ('dp', 'fsdp'))
- smoothed_outputs: float32 [2240, 1024], P(None, ('dp', 'fsdp'))
- velocity_expand: float32 [1024, 4096], P(('dp', 'fsdp'))
- updated_expand: float32 [1024, 4096], P(('dp', 'fsdp'))
- smoothed_expand: float32 [1024, 4096], P(('dp', 'fsdp'))
- velocity_contract: float32 [4096, 1024], P(None, ('dp', 'fsdp'))
- updated_contract: float32 [4096, 1024], P(None, ('dp', 'fsdp'))
- smoothed_contract: float32 [4096, 1024], P(None, ('dp', 'fsdp'))
- velocity_vectors: float32 [4, 1024], P(None, ('dp', 'fsdp'))
- updated_vectors: float32 [4, 1024], P(None, ('dp', 'fsdp'))
- smoothed_vectors: float32 [4, 1024], P(None, ('dp', 'fsdp'))
- velocity_biases: float32 [4992], replicated
- updated_biases: float32 [4992], replicated
- smoothed_biases: float32 [4992], replicated
The draws below stay inside these ranges and needn't reach their ends.
Inputs may be any that keep to these rules, and one draw needn't show every extreme that they name: Each segment counts its first target_counts positions; the last segment counts all 512. `value_routes`: the two experts of one position and head differ. `value_slots`: within one segment and head, the routes to one expert are numbered 0, 1, 2, ... over all first choices in position order and then all second choices; a route numbered 512 or more carries 512 and is dropped; in every segment and head some expert drops routes. `output_routes`: the two experts of one position and head differ. `output_slots`: within one segment and head, the routes to one expert are numbered 0, 1, 2, ... over all first choices in position order and then all second choices; a route numbered 256 or more carries 256 and is dropped; in every segment and head some expert drops routes.
All inputs are finite; a program needn't handle non-finite values.
Results may differ from the reference program's by a relative error of at most 0.0084.
Values may be sent and summed in bfloat16 or wider, within the bound.
No kernel may reach another device: no remote copies, remote signals or barrier semaphores. Data moves between devices by JAX's collectives and lax.ppermute only.
A program may use at most 384 MiB of HBM per device.

```python
import math
import jax
import jax.numpy as jnp
import numpy as np
from jax import lax

D = 1024
H = 4
DH = 112
NE = 5
FF = 4096
V = 8000
SEG = 512
MEM = 512
SEQ_DEV = 1
STEP = 8
SPAN = 1024
CAPV = 512
CAPO = 256
SEQS = 32
PROJ = 936
PARAMS = 22594432
N_DP = 8
N_FSDP = 4


def route_pair(key, row_count, capacity, salt):
    salted = jax.random.fold_in(key, salt)
    subkeys = jax.random.split(salted, 5)
    rotate = jax.random.randint(subkeys[0], (SEQS, H, 1), 0, NE)
    priority = jax.random.randint(subkeys[1], (SEQS, H, row_count), 0, 1 << 20) * row_count + jnp.arange(row_count, dtype=jnp.int32)
    ranking = jnp.argsort(jnp.argsort(priority, axis=-1), axis=-1)
    forced = ranking <= capacity
    draw_low = jax.random.randint(subkeys[2], (SEQS, H, row_count), 0, NE)
    draw_high = jax.random.randint(subkeys[3], (SEQS, H, row_count), 0, NE)
    primary = jnp.where(forced, rotate, (jnp.minimum(draw_low, draw_high) + rotate) % NE)
    secondary = (primary + jax.random.randint(subkeys[4], (SEQS, H, row_count), 1, NE)) % NE
    chosen = jnp.stack([primary, secondary], axis=2)
    onehot = (chosen[..., None] == jnp.arange(NE, dtype=jnp.int32)).astype(jnp.int32)
    flattened = onehot.reshape(SEQS, H, 2 * row_count, NE)
    earlier = jnp.cumsum(flattened, axis=2) - flattened
    ranked = jnp.sum(earlier * flattened, axis=-1).reshape(SEQS, H, 2, row_count)
    capped = jnp.minimum(ranked, capacity)
    return (jnp.transpose(chosen, (0, 3, 1, 2)), jnp.transpose(capped, (0, 3, 1, 2)))


def draw_value_routes(key, part):
    return route_pair(key, SPAN, CAPV, 11)[0]


def draw_value_slots(key, part):
    return route_pair(key, SPAN, CAPV, 11)[1]


def draw_output_routes(key, part):
    return route_pair(key, SEG, CAPO, 13)[0]


def draw_output_slots(key, part):
    return route_pair(key, SEG, CAPO, 13)[1]


def draw_target_counts(key, part):
    key = jax.random.fold_in(key, 31)
    sequence = jnp.arange(SEQS, dtype=jnp.int32)
    device = sequence // SEQ_DEV
    inner_index = device % N_FSDP
    outer_index = device // N_FSDP
    numerator = (N_FSDP - 1 + 2 * inner_index) * (N_DP - 1 + 2 * outer_index)
    denominator = 9 * (N_FSDP - 1) * (N_DP - 1)
    jitter = jax.random.randint(key, (SEQS,), 80, 101)
    jitter = jnp.where(sequence == SEQS - 1, 100, jitter)
    return jnp.maximum(1, SEG * numerator * jitter // (denominator * 100))


def draw_embedding(key, part):
    key = jax.random.fold_in(key, 41)
    row_place = jnp.arange(V, dtype=jnp.float32)[:, None] / (V - 1)
    spread = (1.0 + 2.0 * row_place) * jax.random.normal(key, (V, D), jnp.float32)
    return spread * (1.0 / (1.3 * D ** 0.5))


def draw_vectors(key, part):
    key = jax.random.fold_in(key, 51)
    column = jnp.arange(D, dtype=jnp.float32)[None, :] / (D - 1)
    ramp = 0.5 + column
    jitter = jax.random.normal(key, (4, D), jnp.float32)
    gain_rows = ramp * (1.0 + 0.1 * jitter)
    return jnp.concatenate([gain_rows[:3], 0.3 * jitter[3:]], axis=0)


def place_ends(entries, stream_key, smallest, largest):
    longest = entries.shape.index(max(entries.shape))
    spots = []
    for shift in (0, 1):
        where = [jax.random.randint(jax.random.fold_in(stream_key, axis), (), 0, length) for axis, length in enumerate(entries.shape)]
        where[longest] = (where[longest] + shift) % entries.shape[longest]
        spots.append(tuple(where))
    return entries.at[spots[0]].set(smallest).at[spots[1]].set(largest)


def steps_of(rng, dims, cuts, least, top_value):
    loudness, own = 1.0, jax.random.fold_in(rng, 6)
    for dim, parts in cuts:
        draws = jnp.exp(jax.random.uniform(jax.random.fold_in(own, dim), (parts,), jnp.float32, least / len(cuts), top_value / len(cuts)))
        loudness = loudness * jnp.repeat(draws, dims[dim] // parts).reshape([-1 if axis == dim else 1 for axis in range(len(dims))])
    return loudness


def cumulative_ranks(number_of, skew):
    weights = [(1 << 20) // math.isqrt(rank ** skew) + 1 for rank in range(1, number_of + 1)]
    scale = 1 + sum(weights) // (1 << 30)
    return np.cumsum(np.array([max(1, weight // scale) for weight in weights]))


def skewed_ids(rng, extent, number_of, lean):
    table = cumulative_ranks(number_of, lean)
    ticket = jax.random.randint(jax.random.fold_in(rng, 1), extent, 0, int(table[number_of - 1]))
    rank = jnp.searchsorted(jnp.asarray(table, jnp.int32), ticket, side="right")
    return jax.random.permutation(jax.random.fold_in(rng, 2), number_of)[rank].astype(jnp.int32)


def noise(own_key, dims, deviation, limit, cuts=(), kind=jnp.bfloat16):
    loudness = steps_of(own_key, dims, cuts, -0.22, 0.18) if cuts else 1.0
    array = jax.random.normal(own_key, dims, jnp.float32) * deviation * loudness
    return jnp.minimum(jnp.maximum(array, -limit), limit).astype(kind)


def setup_inputs(seed: int = 0) -> dict:
    key_of = jax.random.split(jax.random.key(seed), 36)
    token_ids = place_ends(skewed_ids(key_of[0], (SEQS, SEG), V, 2), jax.random.fold_in(key_of[0], 3), 0, V - 1).astype(jnp.int32)
    targets = place_ends(skewed_ids(key_of[1], (SEQS, SEG), V, 2), jax.random.fold_in(key_of[1], 3), 0, V - 1).astype(jnp.int32)
    target_counts = draw_target_counts(jax.random.fold_in(key_of[35], 71), 0)
    memory = noise(key_of[3], (SEQS, MEM, D), 1.5, 8.0, ((0, 32),))
    value_routes = draw_value_routes(jax.random.fold_in(key_of[35], 71), 0)
    value_slots = draw_value_slots(jax.random.fold_in(key_of[35], 71), 0)
    output_routes = draw_output_routes(jax.random.fold_in(key_of[35], 71), 0)
    output_slots = draw_output_slots(jax.random.fold_in(key_of[35], 71), 0)
    embedding = draw_embedding(jax.random.fold_in(key_of[35], 71), 0)
    momentum_embedding = noise(key_of[9], (V, D), (0.02 * PARAMS ** -0.5), 2.6702880859375e-05, ((0, 4), (1, 8)), jnp.float32)
    average_embedding = noise(key_of[10], (V, D), D ** -0.5, 0.1875, ((0, 4), (1, 8)), jnp.float32)
    projector = noise(key_of[11], (D, PROJ), (3 * D // 2) ** -0.5, 0.15625, ((0, 32),), jnp.float32)
    momentum_projector = noise(key_of[12], (D, PROJ), (0.02 * PARAMS ** -0.5), 2.6702880859375e-05, ((0, 32),), jnp.float32)
    average_projector = noise(key_of[13], (D, PROJ), (3 * D // 2) ** -0.5, 0.15625, ((0, 32),), jnp.float32)
    position = noise(key_of[14], (D, H * DH), (D // 2) ** -0.5, 0.25, ((0, 32),), jnp.float32)
    momentum_position = noise(key_of[15], (D, H * DH), (0.02 * PARAMS ** -0.5), 2.6702880859375e-05, ((0, 32),), jnp.float32)
    average_position = noise(key_of[16], (D, H * DH), (D // 2) ** -0.5, 0.25, ((0, 32),), jnp.float32)
    values = noise(key_of[17], (D, H * NE * DH), D ** -0.5, 0.1875, ((0, 32),), jnp.float32)
    momentum_values = noise(key_of[18], (D, H * NE * DH), (0.02 * PARAMS ** -0.5), 2.6702880859375e-05, ((0, 32),), jnp.float32)
    average_values = noise(key_of[19], (D, H * NE * DH), D ** -0.5, 0.1875, ((0, 32),), jnp.float32)
    outputs = noise(key_of[20], (H * NE * DH, D), 4 ** -0.5, 3.0, ((1, 32),), jnp.float32)
    momentum_outputs = noise(key_of[21], (H * NE * DH, D), (0.0006 * PARAMS ** -0.5), 7.152557373046875e-07, ((1, 32),), jnp.float32)
    average_outputs = noise(key_of[22], (H * NE * DH, D), 4 ** -0.5, 3.0, ((1, 32),), jnp.float32)
    expand = noise(key_of[23], (D, FF), D ** -0.5, 0.1875, ((0, 32),), jnp.float32)
    momentum_expand = noise(key_of[24], (D, FF), (0.02 * PARAMS ** -0.5), 2.6702880859375e-05, ((0, 32),), jnp.float32)
    average_expand = noise(key_of[25], (D, FF), D ** -0.5, 0.1875, ((0, 32),), jnp.float32)
    contract = noise(key_of[26], (FF, D), (FF // 2) ** -0.5, 0.125, ((1, 32),), jnp.float32)
    momentum_contract = noise(key_of[27], (FF, D), (0.02 * PARAMS ** -0.5), 2.6702880859375e-05, ((1, 32),), jnp.float32)
    average_contract = noise(key_of[28], (FF, D), (FF // 2) ** -0.5, 0.125, ((1, 32),), jnp.float32)
    vectors = draw_vectors(jax.random.fold_in(key_of[35], 71), 0)
    momentum_vectors = noise(key_of[30], (4, D), (0.02 * PARAMS ** -0.5), 2.6702880859375e-05, ((1, 32),), jnp.float32)
    average_vectors = jnp.clip(1.0 + 0.1 * jax.random.normal(key_of[31], (4, D), jnp.float32), 0.5, 1.5)
    biases = noise(key_of[32], (2 * H * DH + FF,), 0.5, 3.0, (), jnp.float32)
    momentum_biases = noise(key_of[33], (2 * H * DH + FF,), (0.02 * PARAMS ** -0.5), 2.6702880859375e-05, (), jnp.float32)
    average_biases = noise(key_of[34], (2 * H * DH + FF,), 0.5, 3.0, (), jnp.float32)
    return {"token_ids": token_ids, "targets": targets, "target_counts": target_counts, "memory": memory, "value_routes": value_routes, "value_slots": value_slots, "output_routes": output_routes, "output_slots": output_slots, "embedding": embedding, "momentum_embedding": momentum_embedding, "average_embedding": average_embedding, "projector": projector, "momentum_projector": momentum_projector, "average_projector": average_projector, "position": position, "momentum_position": momentum_position, "average_position": average_position, "values": values, "momentum_values": momentum_values, "average_values": average_values, "outputs": outputs, "momentum_outputs": momentum_outputs, "average_outputs": average_outputs, "expand": expand, "momentum_expand": momentum_expand, "average_expand": average_expand, "contract": contract, "momentum_contract": momentum_contract, "average_contract": average_contract, "vectors": vectors, "momentum_vectors": momentum_vectors, "average_vectors": average_vectors, "biases": biases, "momentum_biases": momentum_biases, "average_biases": average_biases}


eps = 1e-05
clip_norm = 0.02
momentum_decay = 0.9
rate_base = 10.0
rate_factors = (1.0, 1.0, 1.0, 1.0, 500.0, 1.0, 1.0, 1.0, 8.0)
masked = -1e+30

@jax.custom_vjp
def low(v):
    return lax.optimization_barrier(v.astype(jnp.bfloat16)).astype(jnp.float32)

@jax.custom_vjp
def low_back(v):
    return v

def low_keep(v):
    return (low(v), None)

def low_pass(kept, grad):
    return (grad,)

def back_keep(v):
    return (v, None)

def back_low(kept, grad):
    return (low(grad),)
low.defvjp(low_keep, low_pass)
low_back.defvjp(back_keep, back_low)

def rounded(values):
    return low_back(low(values))

def matmul(left, right):
    return jnp.dot(left, right, precision=lax.Precision.HIGHEST, preferred_element_type=jnp.float32)

def einsum_high(form, left, right):
    return jnp.einsum(form, left, right, precision=lax.Precision.HIGHEST, preferred_element_type=jnp.float32)

def layer_norm(values, gain):
    centred = values - lax.optimization_barrier(jnp.mean(values, axis=-1, keepdims=True))
    return centred * lax.rsqrt(lax.optimization_barrier(jnp.mean(centred * centred, axis=-1, keepdims=True)) + eps) * gain

def positions():
    distances = jnp.arange(SPAN, dtype=jnp.float32)
    freqs = jnp.exp(jnp.arange(D // 2, dtype=jnp.float32) * (-2.0 * math.log(10000.0) / D))
    angles = distances[:, None] * freqs[None, :]
    return jnp.concatenate([jnp.sin(angles), jnp.cos(angles)], axis=1)

def sequence_loss(masters, token_ids, targets, count, memory, value_routes, value_slots, output_routes, output_slots):
    embedding, projector, position, values, outputs, expand, contract, vectors, biases = masters
    table = low(embedding)
    gain_rows = low(vectors)
    head_width = H * DH
    embedded = low_back(table[token_ids] * D ** 0.5)
    stream = jnp.concatenate([memory.astype(jnp.float32), embedded], axis=0)
    normed = rounded(layer_norm(stream, gain_rows[0]))
    projected = matmul(normed, low(projector))
    queries = low_back(projected[MEM:, :head_width])
    key_heads = rounded(projected[:, head_width:2 * head_width]).reshape(SPAN, H, DH)
    value_logits = low_back(projected[:, 2 * head_width:2 * head_width + H * NE])
    output_logits = low_back(projected[MEM:, 2 * head_width + H * NE:])
    rel_keys = rounded(matmul(low(positions()), low(position))).reshape(SPAN, H, DH)
    q_content = rounded(queries + biases[:head_width]).reshape(SEG, H, DH)
    q_position = rounded(queries + biases[head_width:2 * head_width]).reshape(SEG, H, DH)
    every_value = low_back(matmul(normed, low(values))).reshape(SPAN, H, NE, DH)
    value_sigmoid = jax.nn.sigmoid(value_logits).reshape(SPAN, H, NE)
    value_gates = jnp.take_along_axis(value_sigmoid, value_routes, axis=2) * (value_slots < CAPV)
    value_chosen = jnp.take_along_axis(every_value, value_routes[..., None], axis=2)
    mixed_values = rounded(lax.optimization_barrier(jnp.sum(value_gates[..., None] * value_chosen, axis=2)))
    content = low_back(einsum_high('ihd,jhd->hij', q_content, key_heads))
    bias_full = low_back(einsum_high('ihd,rhd->hir', q_position, rel_keys))
    distance = MEM + jnp.arange(SEG)[:, None] - jnp.arange(SPAN)[None, :]
    shift_index = jnp.broadcast_to(jnp.clip(distance, 0, SPAN - 1)[None], (H, SEG, SPAN))
    scores = (content + jnp.take_along_axis(bias_full, shift_index, axis=2)) * DH ** (-0.5)
    scores = jnp.where((distance >= 0)[None], scores, masked)
    attention = rounded(jax.nn.softmax(scores, axis=-1))
    attended = rounded(einsum_high('hij,jhd->ihd', attention, mixed_values))
    out_kernel = low(outputs).reshape(H, NE, DH, D)
    every_output = low_back(einsum_high('ihx,hexd->ihed', attended, out_kernel))
    out_sigmoid = jax.nn.sigmoid(output_logits).reshape(SEG, H, NE)
    out_gates = jnp.take_along_axis(out_sigmoid, output_routes, axis=2) * (output_slots < CAPO)
    out_chosen = jnp.take_along_axis(every_output, output_routes[..., None], axis=2)
    residual = embedded + lax.optimization_barrier(jnp.sum(out_gates[..., None] * out_chosen, axis=(1, 2)))
    normed_mid = rounded(layer_norm(residual, gain_rows[1]))
    hidden = low_back(matmul(normed_mid, low(expand)) + biases[2 * head_width:])
    active = rounded(jax.nn.gelu(hidden, approximate=False))
    final_stream = residual + low_back(matmul(active, low(contract)) + gain_rows[3])
    normed_out = rounded(layer_norm(final_stream, gain_rows[2]))
    logits = low_back(matmul(normed_out, table.T))
    totals = jax.nn.logsumexp(logits, axis=-1)
    picked = jnp.take_along_axis(logits, targets[:, None], axis=1)[:, 0]
    counted = jnp.arange(SEG) < count
    return jnp.sum(jnp.where(counted, totals - picked, 0.0))

def reference(token_ids, targets, target_counts, memory, value_routes, value_slots, output_routes, output_slots, embedding, momentum_embedding, average_embedding, projector, momentum_projector, average_projector, position, momentum_position, average_position, values, momentum_values, average_values, outputs, momentum_outputs, average_outputs, expand, momentum_expand, average_expand, contract, momentum_contract, average_contract, vectors, momentum_vectors, average_vectors, biases, momentum_biases, average_biases):
    masters = (embedding, projector, position, values, outputs, expand, contract, vectors, biases)
    moments = (momentum_embedding, momentum_projector, momentum_position, momentum_values, momentum_outputs, momentum_expand, momentum_contract, momentum_vectors, momentum_biases)
    averages = (average_embedding, average_projector, average_position, average_values, average_outputs, average_expand, average_contract, average_vectors, average_biases)
    sequence_items = (token_ids, targets, target_counts, memory, value_routes, value_slots, output_routes, output_slots)

    def total_loss(weights):

        def one_segment(running, items):
            return (running + jax.checkpoint(sequence_loss)(weights, *items), None)
        summed, unused = lax.scan(one_segment, jnp.zeros((), jnp.float32), sequence_items)
        return summed
    loss_total, pullback = jax.vjp(total_loss, masters)
    gradients, = pullback(jnp.ones((), jnp.float32))
    token_count = jnp.sum(target_counts).astype(jnp.float32)
    gradients = [grad / token_count for grad in gradients]
    squares = jnp.zeros((), jnp.float32)
    for grad in gradients:
        squares = squares + jnp.sum(grad * grad)
    gradient_norm = jnp.sqrt(squares)
    factor = jnp.minimum(1.0, clip_norm / (gradient_norm + 1e-06))
    step_rate = rate_base * (PARAMS / D) ** 0.5
    results = [loss_total, token_count, gradient_norm]
    for weight, velocity, average, grad, multiplier in zip(masters, moments, averages, gradients, rate_factors):
        clipped = grad * factor
        velocity_next = momentum_decay * velocity + clipped
        updated = weight - step_rate * multiplier * (clipped + momentum_decay * velocity_next)
        results = results + [velocity_next, updated, average + (updated - average) / (STEP + 1)]
    return (results[0], results[1], results[2], results[3], results[4], results[5], results[6], results[7], results[8], results[9], results[10], results[11], results[12], results[13], results[14], results[15], results[16], results[17], results[18], results[19], results[20], results[21], results[22], results[23], results[24], results[25], results[26], results[27], results[28], results[29])
```

```python
import functools
import math

import jax
import jax.numpy as jnp
from jax import lax
from jax.experimental import pallas as pl
from jax.experimental.pallas import tpu as pltpu
from jax.sharding import PartitionSpec as P

D = 1024
H = 4
DH = 112
NE = 5
FF = 4096
V = 8000
SEG = 512
MEM = 512
STEP = 8
SPAN = 1024
CAPV = 512
CAPO = 256
HD = H * DH
QUERIES = 2 * HD
VALUE_ROW = 0
OUTPUT_ROW = 2240
QUERY_ROW = 4480
POSITION_ROW = 5376
GATE_ROW = 5824
GATES = 2 * H * NE
LAST_ROWS = 64
PARAMS = 22594432

eps = 1e-05
clip_norm = 0.02
momentum_decay = 0.9
rate_base = 10.0
rate_factors = (1.0, 1.0, 1.0, 1.0, 500.0, 1.0, 1.0, 1.0, 8.0)
masked = -1e30
scale = DH ** (-0.5)
bfloat = jnp.bfloat16
single = jnp.float32
DP, FSDP = "dp", "fsdp"
BOTH = (DP, FSDP)
vmem_bytes = 56 * 1024 * 1024
params = pltpu.CompilerParams(vmem_limit_bytes=vmem_bytes)
light = pl.CostEstimate(flops=10**7, bytes_accessed=10**5, transcendentals=0)


def dot(left, right, left_dim, right_dim):
    return lax.dot_general(
        left, right, (((left_dim,), (right_dim,)), ((), ())), preferred_element_type=single
    )


class Grid:
    def __init__(self):
        self.n_dp = lax.axis_size(DP)
        self.n_fsdp = lax.axis_size(FSDP)
        self.count = self.n_dp * self.n_fsdp
        assert self.count & (self.count - 1) == 0
        self.dp_index = lax.axis_index(DP)
        self.fsdp_index = lax.axis_index(FSDP)
        inner = []
        bit = 2
        while bit < self.n_dp:
            inner.append(bit)
            bit *= 2
        self.layout = ([1] if self.n_dp > 1 else []) + inner[::-1]

        self.sent, self.before = [], ()
        self.summed = []

    def swap(self, part, dp_bits, fsdp_bits=0):
        flip = dp_bits * self.n_fsdp + fsdp_bits
        return lax.ppermute(part, BOTH, [(i, i ^ flip) for i in range(self.count)])

    def queued(self, part, dp_bits, fsdp_bits=0):
        self.sent.append(self.swap(after(part, *self.before), dp_bits, fsdp_bits))
        return self.sent[-1]

    def step(self, *ties):
        self.before, self.sent = tuple(self.sent) + ties, []

    def relative_blocks(self):
        found = [0]
        for bit in self.layout:
            found = [f + b for f in found for b in (0, bit)]
        return found


def after(value, *others):
    return lax.optimization_barrier((value,) + others)[0]


def turn_kernel(in_ref, out_ref):
    out_ref[...] = in_ref[...].T


def turned_block(block):
    rows, columns = block.shape
    return pl.pallas_call(
        turn_kernel,
        grid=(2,),
        in_specs=[pl.BlockSpec((rows, columns // 2), lambda i: (0, i))],
        out_specs=pl.BlockSpec((columns // 2, rows), lambda i: (i, 0)),
        out_shape=jax.ShapeDtypeStruct((columns, rows), block.dtype),
        compiler_params=params,
        cost_estimate=light,
    )(block)


class Gather:
    def __init__(self, grid, shard, turned=False):
        self.grid, self.shard, self.turned = grid, shard, turned

    def direct_line(self):
        grid = self.grid
        self.pieces = [self.shard] + [grid.queued(self.shard, 0, k) for k in range(1, grid.n_fsdp)]
        self.finish_line()

    def first_line(self):
        grid = self.grid
        self.pieces = [self.shard, grid.queued(self.shard, 0, 1)] if grid.n_fsdp > 1 else [self.shard]

    def second_line(self):
        grid = self.grid
        height = self.shard.shape[0]
        bit = 2
        while bit < grid.n_fsdp:
            away = grid.queued(jnp.concatenate(self.pieces, axis=0), 0, bit)
            self.pieces += [away[i * height : (i + 1) * height] for i in range(bit)]
            bit *= 2
        self.finish_line()

    def finish_line(self):
        grid, pieces = self.grid, self.pieces
        bit = 1
        while bit < grid.n_fsdp:
            odd = (grid.fsdp_index & bit) != 0
            pieces = [jnp.where(odd, pieces[i ^ bit], pieces[i]) for i in range(grid.n_fsdp)]
            bit *= 2
        self.line = jnp.concatenate(pieces, axis=0)
        if self.turned:
            self.line = turned_block(self.line)

    def neighbours(self, *ties):
        grid, block = self.grid, after(self.line, *ties)
        self.line = block
        inner = grid.layout[1:]
        self.pieces = [block]
        if len(inner) == 2:
            outer, near = inner
            self.pieces += [grid.queued(block, near), grid.queued(block, outer)]
        else:
            for bit in inner[::-1]:
                self.pieces = [jnp.concatenate(self.pieces, axis=0)]
                self.pieces.append(grid.queued(self.pieces[0], bit))

    def opposite(self, *ties):
        grid = self.grid
        inner = grid.layout[1:]
        if len(inner) == 2:
            outer, near = inner
            middle = self.line.shape[0] // 32 * 16
            self.pieces += [
                grid.queued(after(self.pieces[1][:middle], *ties), outer),
                grid.queued(after(self.pieces[2][middle:], *ties), near),
            ]
        self.own = jnp.concatenate(self.pieces, axis=0)

    def pair(self):
        self.other = self.grid.queued(self.own, 1)

    def rows(self):
        return jnp.concatenate([self.own, self.other], axis=0)

    def by_block(self):
        sides = [side.reshape(-1, *self.line.shape) for side in (self.own, self.other)]
        if self.line.shape[1] % 128:
            sides = [jnp.concatenate(list(side), axis=1)[None] for side in sides]
        return tuple(sides)

    def columns(self):
        count = self.line.shape[0]
        return jnp.concatenate(
            [
                side[i : i + count]
                for side in (self.own, self.other)
                for i in range(0, side.shape[0], count)
            ],
            axis=1,
        )


def opposite_and_neighbours(one, two):
    grid = one.grid
    inner = grid.layout[1:]
    if len(inner) != 2:
        one.opposite()
        two.neighbours()
        return
    outer, near = inner
    middle = one.line.shape[0] // 32 * 16
    first = jnp.concatenate([one.pieces[1][:middle], two.line], axis=0)
    second = jnp.concatenate([one.pieces[2][middle:], two.line], axis=0)
    first, second = grid.queued(first, outer), grid.queued(second, near)
    one.pieces += [first[:middle], second[: one.line.shape[0] - middle]]
    one.own = jnp.concatenate(one.pieces, axis=0)
    two.pieces = [two.line, second[one.line.shape[0] - middle :], first[middle:]]


class Reduce:
    def __init__(self, grid, low, high, columns=False, turned=False):
        self.grid, self.low, self.high = grid, low, high
        self.columns, self.turned = columns, turned

    def pair(self, *ties):
        self.high = self.high(ties).astype(bfloat)
        self.came = self.grid.queued(self.high, 1)
        return self.high

    def opposite(self, *ties):
        grid = self.grid
        total = (self.low(ties) + self.came.astype(single)).astype(bfloat)
        if self.columns:
            width = D // grid.n_dp
            self.blocks = [total[:, i : i + width] for i in range(0, total.shape[1], width)]
        else:
            height = total.shape[0] // (grid.n_dp // 2)
            self.blocks = [total[i : i + height] for i in range(0, total.shape[0], height)]
        inner = grid.layout[1:]
        if len(inner) == 2:
            outer, near = inner
            self.middle = self.blocks[3].shape[0] // 32 * 16
            one, two = self.blocks[3][: self.middle], self.blocks[3][self.middle :]
            self.first, self.second = grid.queued(one, outer), grid.queued(two, near)
            self.met = (self.first, self.second)
            return one, two
        self.met = ()
        return (total,)

    def neighbours(self):
        grid = self.grid
        inner = grid.layout[1:]
        self.sums = []
        if len(inner) == 2:
            outer, near = inner
            rows, middle = self.blocks[0].shape[0], self.middle
            first, second = self.first.astype(single), self.second.astype(single)
            to_near = self.blocks[1].astype(single) + jnp.pad(first, ((0, rows - middle), (0, 0)))
            to_outer = self.blocks[2].astype(single) + jnp.pad(second, ((middle, 0), (0, 0)))
            one, two = to_near.astype(bfloat), to_outer.astype(bfloat)
            self.sums = [grid.queued(one, near), grid.queued(two, outer)]
            total = self.blocks[0].astype(single)
            for part in self.sums:
                total = total + part.astype(single)
            self.block = total.astype(bfloat)
            return one, two
        total = jnp.stack(self.blocks)
        for bit in inner:
            middle = total.shape[0] // 2
            away = grid.queued(total[middle:], bit)
            total = (total[:middle].astype(single) + away.astype(single)).astype(bfloat)
        self.block = total[0]
        return (total,)

    def along_line(self):
        block = self.block.T if self.turned else self.block
        if self.grid.summed:
            block = after(block, self.grid.summed[-1])
        self.shard = lax.psum_scatter(block, FSDP, scatter_dimension=0, tiled=True)
        self.grid.summed.append(self.shard)

    def value(self):
        return self.shard.astype(single)


def total_everywhere(grid, part):
    bit = 1
    while bit < grid.n_dp:
        part = part + grid.swap(part, bit)
        bit *= 2
    bit = 1
    while bit < grid.n_fsdp:
        part = part + grid.swap(part, 0, bit)
        bit *= 2
    return part


def normalised(values):
    centred = values - jnp.mean(values, axis=-1, keepdims=True)
    spread = lax.rsqrt(jnp.mean(centred * centred, axis=-1, keepdims=True) + eps)
    return centred * spread, spread


def norm_gradient(grad, normal, spread, gain):
    scaled = grad * gain
    mean_one = jnp.mean(scaled, axis=-1, keepdims=True)
    mean_two = jnp.mean(scaled * normal, axis=-1, keepdims=True)
    return spread * (scaled - mean_one - normal * mean_two), jnp.sum(grad * normal, axis=0)


def gelu_exact(values):
    return jax.nn.gelu(values, approximate=False)


def positions(length, features):
    distances = jnp.arange(length, dtype=single)[::-1]
    freqs = jnp.exp(jnp.arange(features // 2, dtype=single) * (-2.0 * math.log(10000.0) / features))
    angles = distances[:, None] * freqs[None, :]
    return jnp.concatenate([jnp.sin(angles), jnp.cos(angles)], axis=1)


def lanes(*sides):
    return jnp.concatenate([side[i] for side in sides for i in range(side.shape[0])], axis=1)


def sums_of_experts(gates, blocks):
    return sum(gates[e : e + 1] * blocks[e * DH : (e + 1) * DH] for e in range(NE))


def each_expert(gates, block):
    return jnp.concatenate([gates[e : e + 1] * block for e in range(NE)], axis=0).astype(bfloat)


def expert_products(blocks, block):
    sums = [
        jnp.sum(blocks[e * DH : (e + 1) * DH].astype(single) * block, axis=0, keepdims=True)
        for e in range(NE)
    ]
    return jnp.concatenate(sums + [jnp.zeros_like(sums[0])] * (8 - NE), axis=0)


def mix_kernel(*refs):
    normed, rel, *sides = refs[:12]
    content_ref, position_ref, value_gate, output_gate = refs[12:16]
    qa_ref, qb_ref, k_ref, r_ref, v_ref, o_ref, p_ref, every_ref, gated_ref, out_ref = refs[16:]
    query, key, far, value, output = (lanes(*sides[i : i + 2]) for i in range(0, 10, 2))
    queries = dot(query, normed[MEM:, :], 1, 1)
    qa_ref[0] = (queries + content_ref[0]).astype(bfloat)
    qb_ref[0] = (queries + position_ref[0]).astype(bfloat)
    k_ref[0] = dot(key, normed[...], 1, 1).astype(bfloat)
    r_ref[0] = dot(far, rel[...], 1, 1).astype(bfloat)
    every = dot(value, normed[...], 1, 1)
    every_ref[0] = every.astype(bfloat)
    v_ref[0] = sums_of_experts(value_gate[0], every).astype(bfloat)
    bias = dot(qb_ref[0], r_ref[0], 0, 0)
    bias = pltpu.roll(bias, SPAN - SEG + 1, 1, stride=1, stride_axis=0)
    row = lax.broadcasted_iota(jnp.int32, (SEG, SPAN), 0)
    column = lax.broadcasted_iota(jnp.int32, (SEG, SPAN), 1)
    scores = (dot(qa_ref[0], k_ref[0], 0, 0) + bias) * scale
    scores = jnp.where(column <= MEM + row, scores, masked)
    powers = jnp.exp(scores - jnp.max(scores, axis=1, keepdims=True))
    weights = powers / jnp.sum(powers, axis=1, keepdims=True)
    p_ref[0] = weights
    attended = dot(v_ref[0], weights.astype(bfloat), 1, 1).astype(bfloat)
    o_ref[0] = attended
    gated = each_expert(output_gate[0], attended.astype(single))
    gated_ref[0] = gated

    @pl.when(pl.program_id(0) == 0)
    def _():
        out_ref[...] = jnp.zeros_like(out_ref)

    out_ref[...] += dot(gated, output, 0, 0)


def mix_back_kernel(*refs):
    grad_ref, *sides = refs[:9]
    qa_ref, qb_ref, k_ref, r_ref, v_ref, o_ref, p_ref, every_ref, value_gate, output_gate = refs[9:19]
    dq_ref, dk_ref, dr_ref, dv_ref, dzv_ref, dzo_ref, du_ref, dw_ref, out_ref = refs[19:]
    query, key, value, output = (lanes(*sides[i : i + 2]) for i in range(0, 8, 2))
    back = dot(output, grad_ref[...], 1, 1)
    gate = output_gate[0]
    dzo_ref[0] = expert_products(back, o_ref[0].astype(single)) * gate * (1.0 - gate)
    grad_out = sums_of_experts(gate, back).astype(bfloat)
    weights = p_ref[0]
    grad_mixed = dot(grad_out, weights.astype(bfloat), 1, 0).astype(bfloat).astype(single)
    grad = dot(grad_out, v_ref[0], 0, 0).astype(bfloat).astype(single)
    grad = weights * (grad - jnp.sum(grad * weights, axis=1, keepdims=True)) * scale
    low = grad.astype(bfloat)
    grad_qa = dot(k_ref[0], low, 1, 1).astype(bfloat).astype(single)
    grad_key = dot(qa_ref[0], low, 1, 0).astype(bfloat)
    row = lax.broadcasted_iota(jnp.int32, (SEG, SEG), 0)
    column = lax.broadcasted_iota(jnp.int32, (SEG, SEG), 1)
    turn = jnp.where(row + column == SEG - 1, 1.0, 0.0).astype(bfloat)
    far = pltpu.roll(dot(turn, low, 1, 0), 0, 1, stride=1, stride_axis=0).astype(bfloat)
    dr_ref[0] = dot(dot(qb_ref[0], turn, 1, 0).astype(bfloat), far, 1, 0).astype(bfloat)
    grad_qb = dot(dot(r_ref[0], far, 1, 1).astype(bfloat), turn, 1, 0)
    du_ref[0] = jnp.sum(grad_qa, axis=1, keepdims=True)
    dw_ref[0] = jnp.sum(grad_qb, axis=1, keepdims=True)
    grad_query = (grad_qa + grad_qb).astype(bfloat)
    dq_ref[0, :, :MEM] = jnp.zeros((DH, MEM), bfloat)
    dq_ref[0, :, MEM:] = grad_query
    dk_ref[0] = grad_key
    gate = value_gate[0]
    dzv_ref[0] = expert_products(every_ref[0], grad_mixed) * gate * (1.0 - gate)
    grad_value = each_expert(gate, grad_mixed)
    dv_ref[0] = grad_value

    @pl.when(pl.program_id(0) == 0)
    def _():
        out_ref[...] = jnp.zeros_like(out_ref)

    out_ref[...] += dot(grad_key, key, 0, 0) + dot(grad_value, value, 0, 0)
    out_ref[MEM:, :] += dot(grad_query, query, 0, 0)


def head_rows(rows, columns, dtype=bfloat):
    block = pl.BlockSpec((1, rows, columns), lambda h: (h, 0, 0))
    return block, jax.ShapeDtypeStruct((H, rows, columns), dtype)


def weight_blocks(sides, start, rows):
    blocks, _, width = sides[0].shape
    return [pl.BlockSpec((blocks, rows, width), lambda h: (0, start // rows + h, 0))] * 2


def fixed(rows, columns):
    return pl.BlockSpec((rows, columns), lambda *_: (0, 0))


EXPERT = NE * DH


def mix(normed, rel, sides, content, position, value_gates, output_gates):
    outs = [
        head_rows(DH, SEG),
        head_rows(DH, SEG),
        head_rows(DH, SPAN),
        head_rows(DH, SPAN),
        head_rows(DH, SPAN),
        head_rows(DH, SEG),
        head_rows(SEG, SPAN, single),
        head_rows(EXPERT, SPAN),
        head_rows(EXPERT, SEG),
        (fixed(SEG, D), jax.ShapeDtypeStruct((SEG, D), single)),
    ]
    return pl.pallas_call(
        mix_kernel,
        grid=(H,),
        in_specs=[fixed(SPAN, D), fixed(SPAN, D)]
        + weight_blocks(sides, QUERY_ROW, DH)
        + weight_blocks(sides, QUERY_ROW + HD, DH)
        + weight_blocks(sides, POSITION_ROW, DH)
        + weight_blocks(sides, VALUE_ROW, EXPERT)
        + weight_blocks(sides, OUTPUT_ROW, EXPERT)
        + [head_rows(DH, 1)[0]] * 2
        + [head_rows(8, SPAN)[0], head_rows(8, SEG)[0]],
        out_specs=[spec for spec, _ in outs],
        out_shape=[shape for _, shape in outs],
        compiler_params=params,
        cost_estimate=light,
    )(normed, rel, *(sides * 5), content, position, value_gates, output_gates)


def mix_back(grad, sides, stored, value_gates, output_gates):
    outs = [
        head_rows(DH, SPAN),
        head_rows(DH, SPAN),
        head_rows(DH, SPAN),
        head_rows(EXPERT, SPAN),
        head_rows(8, SPAN, single),
        head_rows(8, SEG, single),
        head_rows(DH, 1, single),
        head_rows(DH, 1, single),
        (fixed(SPAN, D), jax.ShapeDtypeStruct((SPAN, D), single)),
    ]
    return pl.pallas_call(
        mix_back_kernel,
        grid=(H,),
        in_specs=[fixed(SEG, D)]
        + weight_blocks(sides, QUERY_ROW, DH)
        + weight_blocks(sides, QUERY_ROW + HD, DH)
        + weight_blocks(sides, VALUE_ROW, EXPERT)
        + weight_blocks(sides, OUTPUT_ROW, EXPERT)
        + [head_rows(*array.shape[1:])[0] for array in stored]
        + [head_rows(8, SPAN)[0], head_rows(8, SEG)[0]],
        out_specs=[spec for spec, _ in outs],
        out_shape=[shape for _, shape in outs],
        compiler_params=params,
        cost_estimate=light,
    )(grad, *(sides * 4), *stored, value_gates, output_gates)


ff_tile = 512
ff_columns = pl.BlockSpec((SEG, ff_tile), lambda i: (0, i))
ff_weights = pl.BlockSpec((D // 2, ff_tile), lambda i: (0, i))
ff_bias = pl.BlockSpec((1, ff_tile), lambda i: (0, i))


def expand_kernel(in_ref, own_ref, other_ref, bias_ref, act_ref, slope_ref):
    hidden = dot(in_ref[:, : D // 2], own_ref[...], 1, 0) + bias_ref[...]
    hidden = hidden + dot(in_ref[:, D // 2 :], other_ref[...], 1, 0)
    share = 0.5 + 0.5 * lax.erf(hidden * math.sqrt(0.5))
    act_ref[...] = (hidden * share).astype(bfloat)
    density = jnp.exp(hidden * hidden * -0.5) * (1.0 / math.sqrt(2.0 * math.pi))
    slope_ref[...] = (share + hidden * density).astype(bfloat)


def expand_forward(normed, sides, bias):
    wide = jax.ShapeDtypeStruct((SEG, FF), bfloat)
    return pl.pallas_call(
        expand_kernel,
        grid=(FF // ff_tile,),
        in_specs=[fixed(SEG, D), ff_weights, ff_weights, ff_bias],
        out_specs=[ff_columns, ff_columns],
        out_shape=[wide, wide],
        compiler_params=params,
        cost_estimate=light,
    )(normed, *sides, bias)


def contract_kernel(act_ref, own_ref, other_ref, out_ref):
    @pl.when(pl.program_id(0) == 0)
    def _():
        out_ref[...] = jnp.zeros_like(out_ref)

    out_ref[:, : D // 2] += dot(act_ref[...], own_ref[...], 1, 1)
    out_ref[:, D // 2 :] += dot(act_ref[...], other_ref[...], 1, 1)


def contract_forward(active, sides):
    return pl.pallas_call(
        contract_kernel,
        grid=(FF // ff_tile,),
        in_specs=[ff_columns, ff_weights, ff_weights],
        out_specs=fixed(SEG, D),
        out_shape=jax.ShapeDtypeStruct((SEG, D), single),
        compiler_params=params,
        cost_estimate=light,
    )(active, *sides)


def ff_back_kernel(
    in_ref, slope_ref, own_down, other_down, own_up, other_up, grad_ref, bias_ref, out_ref, total
):
    tile = pl.program_id(0)

    @pl.when(tile == 0)
    def _():
        total[...] = jnp.zeros_like(total)

    grad = dot(in_ref[:, : D // 2], own_down[...], 1, 0)
    grad = grad + dot(in_ref[:, D // 2 :], other_down[...], 1, 0)
    grad = grad.astype(bfloat).astype(single) * slope_ref[...].astype(single)
    low = grad.astype(bfloat)
    grad_ref[...] = low
    bias_ref[...] = jnp.sum(low.astype(single), axis=0, keepdims=True)
    total[:, : D // 2] += dot(low, own_up[...], 1, 1)
    total[:, D // 2 :] += dot(low, other_up[...], 1, 1)

    @pl.when(tile == pl.num_programs(0) - 1)
    def _():
        out_ref[...] = total[...].astype(bfloat)


def ff_back(grad, slope, down, up):
    return pl.pallas_call(
        ff_back_kernel,
        grid=(FF // ff_tile,),
        in_specs=[fixed(SEG, D), ff_columns] + [ff_weights] * 4,
        out_specs=[ff_columns, ff_bias, fixed(SEG, D)],
        out_shape=[
            jax.ShapeDtypeStruct((SEG, FF), bfloat),
            jax.ShapeDtypeStruct((1, FF), single),
            jax.ShapeDtypeStruct((SEG, D), bfloat),
        ],
        scratch_shapes=[pltpu.VMEM((SEG, D), single)],
        compiler_params=params,
        cost_estimate=light,
    )(grad, slope, *down, *up)


def lookup_kernel(first, ids_ref, own_ref, other_ref, out_ref):
    tile = pl.program_id(0)
    rows = own_ref.shape[1]
    place = first + tile * rows + lax.broadcasted_iota(jnp.int32, (SEG, rows), 1)
    chosen = jnp.where(ids_ref[...] == place, 1.0, 0.0).astype(bfloat)
    found = dot(chosen, lanes(own_ref, other_ref), 1, 0)

    @pl.when(tile == 0)
    def _():
        out_ref[...] = found

    @pl.when(tile > 0)
    def _():
        out_ref[...] += found


def lookup(ids, own, other, first):
    blocks, rows, width = own.shape
    tile = 1024
    side = pl.BlockSpec((blocks, tile, width), lambda i: (0, i, 0))
    return pl.pallas_call(
        functools.partial(lookup_kernel, first),
        grid=(rows // tile,),
        in_specs=[pl.BlockSpec((SEG, 1), lambda i: (0, 0)), side, side],
        out_specs=pl.BlockSpec((SEG, D), lambda i: (0, 0)),
        out_shape=jax.ShapeDtypeStruct((SEG, D), single),
        compiler_params=params,
        cost_estimate=light,
    )(ids, own, other)


head_tile = 512


def head_kernel(
    shard_rows,
    shard_half,
    hf_ref,
    goal_ref,
    counted_ref,
    own_zero,
    other_zero,
    own_one,
    other_one,
    grad_ref,
    back_ref,
    loss_ref,
    logits,
    total,
    highest,
    summed,
    picked,
):
    tiles = pl.num_programs(0) // 2
    step = pl.program_id(0)
    tile = lax.rem(step, tiles)
    at = pl.multiple_of(tile * head_tile, head_tile)
    place = at + lax.broadcasted_iota(jnp.int32, (SEG, head_tile), 1)
    hits = place == goal_ref[...]

    def each_table(use):
        @pl.when(tile < tiles // 2)
        def _():
            use(lanes(own_zero, other_zero), 0)

        @pl.when(tile >= tiles // 2)
        def _():
            use(lanes(own_one, other_one), shard_half)

    def groups(values):
        return [values[:, i : i + 128] for i in range(0, head_tile, 128)]

    @pl.when(step == 0)
    def _():
        highest[...] = jnp.full_like(highest, masked)
        summed[...] = jnp.zeros_like(summed)
        picked[...] = jnp.zeros_like(picked)
        total[...] = jnp.zeros_like(total)

    @pl.when(step < tiles)
    def _():
        def use(rows, late):
            scores = dot(hf_ref[...], rows, 1, 1)
            scores = jnp.where(lax.rem(place, shard_half) + late < shard_rows, scores, masked)
            logits[:, pl.ds(at, head_tile)] = scores
            parts = groups(scores)
            top = functools.reduce(jnp.maximum, parts, highest[...])
            powers = sum(jnp.exp(part - top) for part in parts)
            summed[...] = summed[...] * jnp.exp(highest[...] - top) + powers
            highest[...] = top
            picked[...] += sum(groups(jnp.where(hits, scores, 0.0)))

        each_table(use)

    @pl.when(step == tiles)
    def _():
        top = jnp.max(highest[...], axis=1, keepdims=True)
        powers = jnp.sum(summed[...] * jnp.exp(highest[...] - top), axis=1, keepdims=True)
        whole = top + jnp.log(powers)
        loss_ref[...] = (whole - jnp.sum(picked[...], axis=1, keepdims=True)) * counted_ref[...]
        highest[...] = jnp.broadcast_to(whole, highest.shape)

    @pl.when(step >= tiles)
    def _():
        def use(rows, late):
            shares = jnp.exp(logits[:, pl.ds(at, head_tile)] - highest[:, :1])
            grad = ((shares - jnp.where(hits, 1.0, 0.0)) * counted_ref[...]).astype(bfloat)
            grad_ref[...] = grad
            total[...] += dot(grad, rows, 1, 0)

        each_table(use)

    @pl.when(step == 2 * tiles - 1)
    def _():
        back_ref[...] = total[...].astype(bfloat)


def head(hf, goals, counted, parts, shard_rows, shard_half):
    blocks, rows, width = parts[0][0].shape
    half_tiles = rows // head_tile
    tiles = 2 * half_tiles

    def side(part):
        def index(i):
            return 0, jnp.clip(lax.rem(i, tiles) - part * half_tiles, 0, half_tiles - 1), 0

        return pl.BlockSpec((blocks, head_tile, width), index)

    column = pl.BlockSpec((SEG, 1), lambda i: (0, 0))
    whole = pl.BlockSpec((SEG, D), lambda i: (0, 0))
    return pl.pallas_call(
        functools.partial(head_kernel, shard_rows, shard_half),
        grid=(2 * tiles,),
        in_specs=[whole, column, column, side(0), side(0), side(1), side(1)],
        out_specs=[
            pl.BlockSpec((SEG, head_tile), lambda i: (0, jnp.maximum(i - tiles, 0))),
            whole,
            column,
        ],
        out_shape=[
            jax.ShapeDtypeStruct((SEG, 2 * rows), bfloat),
            jax.ShapeDtypeStruct((SEG, D), bfloat),
            jax.ShapeDtypeStruct((SEG, 1), single),
        ],
        scratch_shapes=[
            pltpu.VMEM((SEG, 2 * rows), single),
            pltpu.VMEM((SEG, D), single),
            pltpu.VMEM((SEG, 128), single),
            pltpu.VMEM((SEG, 128), single),
            pltpu.VMEM((SEG, 128), single),
        ],
        compiler_params=params,
        cost_estimate=light,
    )(hf, goals, counted, *parts[0], *parts[1])


def chosen_experts(routes, slots, capacity):
    experts = jnp.arange(NE, dtype=jnp.int32)[None, :, None, None]
    turned = jnp.transpose(routes, (1, 2, 0))[:, None]
    kept = jnp.transpose(slots, (1, 2, 0))[:, None] < capacity
    return jnp.sum(((turned == experts) & kept).astype(single), axis=2)


def advance(weight, velocity, average, grad, factor, step_rate):
    clipped = grad * factor
    velocity_next = momentum_decay * velocity + clipped
    updated = weight - step_rate * (clipped + momentum_decay * velocity_next)
    return (velocity_next, updated, average + (updated - average) / (STEP + 1))


def table_shape(grid):
    rows = V // grid.n_fsdp
    return rows, -(-rows // 256) * 128


def table_place(grid, ids):
    rows, part = table_shape(grid)
    owner, row = ids // rows, ids % rows
    return (row // part) * (grid.n_fsdp * part) + owner * part + row % part


def body(
    token_ids,
    targets,
    target_counts,
    memory,
    value_routes,
    value_slots,
    output_routes,
    output_slots,
    *states,
):
    masters, moments, averages = states[0::3], states[1::3], states[2::3]
    embedding, projector, position, values, outputs, expand, contract, vectors, biases = masters
    grid = Grid()
    ids = table_place(grid, token_ids[0])
    goals = table_place(grid, targets[0])
    half = D // 2
    chunk = D // grid.count

    shard_rows, shard_half = table_shape(grid)
    part_rows = shard_half * grid.n_fsdp
    table_shard = jnp.pad(embedding.astype(bfloat), ((0, 2 * shard_half - shard_rows), (0, 0)))
    expanding = Gather(grid, expand.astype(bfloat))
    contracting = Gather(grid, contract.T.astype(bfloat))
    tables = [Gather(grid, table_shard[i : i + shard_half]) for i in (0, shard_half)]
    attention_shard = jnp.concatenate(
        [
            values.astype(bfloat),
            outputs.T.astype(bfloat),
            projector[:, :QUERIES].astype(bfloat),
            position.astype(bfloat),
            projector[:, QUERIES:].astype(bfloat),
            vectors.T.astype(bfloat),
            jnp.zeros((chunk, LAST_ROWS - GATES - 4), bfloat),
        ],
        axis=1,
    )
    attending = Gather(grid, attention_shard, True)
    distances = jnp.array(grid.relative_blocks(), jnp.int32)
    width = D // grid.n_dp
    true_columns = (
        (distances[:, None] ^ grid.dp_index) * width + jnp.arange(width, dtype=jnp.int32)[None, :]
    ).reshape(D)
    to_order = (jnp.arange(D, dtype=jnp.int32)[:, None] == true_columns[None, :]).astype(bfloat)
    memory_rows = dot(memory[0], to_order, 1, 0)
    rel_table = dot(positions(SPAN, D).astype(bfloat), to_order, 1, 0).astype(bfloat)

    tables[0].direct_line()
    grid.step(memory_rows, rel_table)
    tables[0].neighbours()
    tables[1].direct_line()
    grid.step()
    opposite_and_neighbours(tables[0], tables[1])
    attending.direct_line()
    grid.step()
    middle = expand.shape[1]
    lines = lax.all_gather(
        after(jnp.concatenate([expanding.shard, contracting.shard], axis=1), *grid.before),
        FSDP,
        axis=0,
        tiled=True,
    )
    expanding.line, contracting.line = lines[:, :middle], lines[:, middle:]
    tables[1].opposite()
    tables[0].pair()
    attending.neighbours()
    grid.step()
    attending.opposite()
    expanding.neighbours()
    tables[1].pair()
    tables_by_block = [part.by_block() for part in tables]
    found = [lookup(ids[:, None], *tables_by_block[0], 0)]
    grid.step(found[0])
    attending.pair()
    expanding.opposite()
    contracting.neighbours()
    found.append(lookup(ids[:, None], *tables_by_block[1], part_rows))
    embedded = (found[0] + found[1]) * D**0.5
    grid.step(embedded)
    contracting.opposite()
    expanding.pair()
    grid.step()
    contracting.pair()
    attention = attending.by_block()
    last_rows = jnp.concatenate(
        [side[i, GATE_ROW:] for side in attention for i in range(side.shape[0])], axis=1
    )
    gains = last_rows[GATES : GATES + 4].astype(single)

    stream = jnp.concatenate([memory_rows, embedded], axis=0)
    normal_in, spread_in = normalised(stream)
    normed = (normal_in * gains[0]).astype(bfloat)
    logits = jax.nn.sigmoid(dot(last_rows, normed, 1, 1)[:GATES])

    def gates_of(shares, routes, slots, capacity):
        kept = shares.reshape(H, NE, -1) * chosen_experts(routes, slots, capacity)
        return jnp.pad(kept, ((0, 0), (0, 8 - NE), (0, 0)))

    value_gates = gates_of(logits[: H * NE], value_routes[0], value_slots[0], CAPV)
    output_gates = gates_of(logits[H * NE :, MEM:], output_routes[0], output_slots[0], CAPO)
    *stored, gated, mixed = mix(
        normed,
        rel_table,
        attention,
        biases[:HD].reshape(H, DH, 1),
        biases[HD : 2 * HD].reshape(H, DH, 1),
        value_gates,
        output_gates,
    )
    gated = gated.reshape(H * EXPERT, SEG)
    residual = embedded + mixed
    normal_mid, spread_mid = normalised(residual)
    normed_mid = (normal_mid * gains[1]).astype(bfloat)
    up, down = (expanding.own, expanding.other), (contracting.own, contracting.other)
    active, slope = expand_forward(normed_mid, up, biases[None, 2 * HD :])
    final = residual + contract_forward(active, down) + gains[3]
    normal_out, spread_out = normalised(final)
    normed_out = (normal_out * gains[2]).astype(bfloat)

    counted = (jnp.arange(SEG, dtype=jnp.int32) < target_counts[0]).astype(single)
    grad_logits, grad_out, losses = head(
        normed_out, goals[:, None], counted[:, None], tables_by_block, shard_rows, shard_half
    )
    loss = jnp.sum(losses)

    grad_final, grad_gain_out = norm_gradient(
        grad_out.astype(single), normal_out, spread_out, gains[2]
    )
    grad_branch = grad_final.astype(bfloat)
    grad_bias_down = jnp.sum(grad_branch.astype(single), axis=0)

    def summing(wide, other, wide_dim, other_dim):
        def part(start):
            side = lax.slice_in_dim(wide, start, start + half, axis=1)
            return lambda ties: dot(after(side, *ties), other, wide_dim, other_dim)

        return Reduce(grid, part(0), part(half))

    def summing_turned(wide, other):
        def part(start):
            side = lax.slice_in_dim(wide, start, start + half, axis=1)
            return lambda ties: dot(other, after(side, *ties), 1, 0)

        return Reduce(grid, part(0), part(half), True, True)

    grid.step()
    contracting = summing(grad_branch, active, 0, 0)
    tie = contracting.pair()
    grad_hidden, grad_bias_up, grad_mid = ff_back(after(grad_branch, tie), slope, down, up)
    expanding = summing(normed_mid, grad_hidden, 0, 0)
    tie = expanding.pair()
    tie_two = contracting.opposite()
    grad_mid = after(grad_mid, tie, *tie_two)
    grad_residual, grad_gain_mid = norm_gradient(
        grad_mid.astype(single), normal_mid, spread_mid, gains[1]
    )
    grad_residual = grad_residual + grad_final
    low_residual = grad_residual.astype(bfloat)
    outputting = summing_turned(low_residual, gated)
    tie = outputting.pair()
    tie_two = expanding.opposite()
    tie_three = contracting.neighbours()
    tie_four = outputting.opposite()
    (
        grad_queries,
        grad_keys,
        grad_rel,
        grad_values,
        grad_value_gates,
        grad_output_gates,
        grad_content,
        grad_position,
        grad_normed,
    ) = mix_back(
        after(low_residual, *tie_two, *tie_three, *tie_four),
        attention,
        stored,
        value_gates,
        output_gates,
    )
    tie = expanding.neighbours()
    grad_values = grad_values.reshape(H * EXPERT, SPAN)
    grad_gates = jnp.concatenate(
        [
            grad_value_gates[:, :NE].reshape(H * NE, SPAN),
            jnp.pad(grad_output_gates[:, :NE].reshape(H * NE, SEG), ((0, 0), (MEM, 0))),
            jnp.zeros((LAST_ROWS - GATES, SPAN), single),
        ],
        axis=0,
    ).astype(bfloat)
    contracting.along_line()
    tie = outputting.neighbours()
    grad_normed = (grad_normed + dot(grad_gates, last_rows, 0, 0)).astype(bfloat)
    grad_normed = after(grad_normed, *expanding.sums)
    expanding.along_line()
    grad_stream, grad_gain_in = norm_gradient(
        grad_normed.astype(single), normal_in, spread_in, gains[0]
    )
    grad_embedded = (grad_residual + grad_stream[MEM:]).astype(bfloat)
    nothing = jnp.zeros((D,), single)
    grad_vectors = jnp.stack(
        [nothing] * GATES
        + [grad_gain_in, grad_gain_mid, grad_gain_out, grad_bias_down]
        + [nothing] * (LAST_ROWS - GATES - 4)
    )

    tokens = jnp.arange(2 * part_rows, dtype=jnp.int32)[None, :]
    looked = (ids[:, None] == tokens).astype(bfloat)
    table_left = jnp.concatenate([grad_logits, looked], axis=0)
    table_right = jnp.concatenate([normed_out, grad_embedded * bfloat(D**0.5)], axis=0)

    def table_summing(start):
        side = table_left[:, start : start + part_rows]

        def part(column):
            right = table_right[:, column : column + half]
            return lambda ties: dot(side, after(right, *ties), 0, 0)

        return Reduce(grid, part(0), part(half), columns=True)

    tables = [table_summing(i) for i in (0, part_rows)]
    valuing = summing_turned(normed, grad_values)

    def small_half(start):
        def compute(ties):
            stop = start + half
            side = after(normed[:, start:stop], *ties)
            return jnp.concatenate(
                [
                    dot(grad_queries.reshape(HD, SPAN), side, 1, 0),
                    dot(grad_keys.reshape(HD, SPAN), side, 1, 0),
                    dot(grad_rel.reshape(HD, SPAN), rel_table[:, start:stop], 1, 0),
                    dot(grad_gates, side, 1, 0) + grad_vectors[:, start:stop],
                ],
                axis=0,
            )

        return compute

    smalling = Reduce(grid, small_half(0), small_half(half), True, True)
    tie = tables[0].pair(contracting.shard)
    tie = tables[1].pair(tie)
    outputting.along_line()
    tie = tables[0].opposite(tie, *outputting.sums, expanding.shard)
    tie = (valuing.pair(*tie),)
    tie = tables[1].opposite(*tie)
    tie = tables[0].neighbours() + tie
    tie = (smalling.pair(*tie, outputting.shard),)
    tie = valuing.opposite(*tie, *tables[1].met)
    tie = tables[1].neighbours() + tie
    tables[0].along_line()
    tie = smalling.opposite(*tie)
    valuing.neighbours()
    tables[1].along_line()
    smalling.neighbours()
    valuing.along_line()
    smalling.along_line()
    sum_contract, sum_expand, sum_outputs, sum_values, sum_small = (
        part.value() for part in (contracting, expanding, outputting, valuing, smalling)
    )
    sum_table = jnp.concatenate([part.value() for part in tables], axis=0)[:shard_rows]

    shard_grads = [
        sum_table,
        jnp.concatenate([sum_small[:, :QUERIES], sum_small[:, 3 * HD : 3 * HD + GATES]], axis=1),
        sum_small[:, QUERIES : 3 * HD],
        sum_values,
        sum_outputs.T,
        sum_expand,
        sum_contract.T,
        sum_small[:, 3 * HD + GATES : 3 * HD + GATES + 4].T,
    ]
    most_tokens = grid.count * SEG
    local_squares = jnp.zeros((), single)
    for grad in shard_grads:
        scaled = grad * (1.0 / most_tokens)
        local_squares = local_squares + jnp.sum(scaled * scaled)
    shared = jnp.concatenate(
        [
            grad_content.reshape(HD),
            grad_position.reshape(HD),
            grad_bias_up.reshape(FF),
            jnp.stack([loss, target_counts[0].astype(single), local_squares]),
        ]
    )
    shared = total_everywhere(grid, shared)
    bias_grad, loss_total, token_count, squares = shared[:-3], shared[-3], shared[-2], shared[-1]
    scaled = bias_grad * (1.0 / most_tokens)
    gradient_norm = jnp.sqrt(squares + jnp.sum(scaled * scaled)) * (most_tokens / token_count)
    factor = jnp.minimum(1.0, clip_norm / (gradient_norm + 1e-06))
    inverse = 1.0 / token_count
    shard_grads = [grad * inverse for grad in shard_grads]
    bias_grad = bias_grad * inverse
    step_rate = rate_base * (PARAMS / D) ** 0.5
    results = (loss_total, token_count, gradient_norm)
    for weight, velocity, average, grad, multiplier in zip(
        masters, moments, averages, shard_grads + [bias_grad], rate_factors
    ):
        results += advance(weight, velocity, average, grad, factor, step_rate * multiplier)
    return results


def solution(mesh):
    batch = P(BOTH)
    rows, columns, whole = P(BOTH, None), P(None, BOTH), P()
    kinds = (P(FSDP, DP), rows, rows, rows, columns, rows, columns, columns, whole)
    triples = tuple(kind for kind in kinds for _ in range(3))
    return jax.shard_map(
        body,
        mesh=mesh,
        in_specs=(batch,) * 8 + triples,
        out_specs=(whole,) * 3 + triples,
        check_vma=False,
    )
```

```python
import functools
import math

import jax
import jax.numpy as jnp
from jax import lax
from jax.experimental import pallas as pl
from jax.experimental.pallas import tpu as pltpu
from jax.sharding import PartitionSpec as P

D = 1024
H = 4
DH = 112
NE = 5
FF = 4096
V = 8000
SEG = 512
MEM = 512
STEP = 8
SPAN = 1024
CAPV = 512
CAPO = 256
HD = H * DH
QUERIES = 2 * HD
VALUE_ROW = 0
OUTPUT_ROW = 2240
QUERY_ROW = 4480
POSITION_ROW = 5376
GATE_ROW = 5824
GATES = 2 * H * NE
LAST_ROWS = 64
PARAMS = 22594432

eps = 1e-05
clip_norm = 0.02
momentum_decay = 0.9
rate_base = 10.0
rate_factors = (1.0, 1.0, 1.0, 1.0, 500.0, 1.0, 1.0, 1.0, 8.0)
masked = -1e30
scale = DH ** (-0.5)
bfloat = jnp.bfloat16
single = jnp.float32
DP, FSDP = "dp", "fsdp"
BOTH = (DP, FSDP)
vmem_bytes = 56 * 1024 * 1024
params = pltpu.CompilerParams(vmem_limit_bytes=vmem_bytes)
light = pl.CostEstimate(flops=10**7, bytes_accessed=10**5, transcendentals=0)


def dot(left, right, left_dim, right_dim):
    return lax.dot_general(
        left, right, (((left_dim,), (right_dim,)), ((), ())), preferred_element_type=single
    )


class Sent:
    def __init__(self, value):
        self.value = value


def came(*parts):
    return [part.value if isinstance(part, Sent) else part for part in parts]


class Grid:
    def __init__(self):
        self.n_dp = lax.axis_size(DP)
        self.n_fsdp = lax.axis_size(FSDP)
        self.count = self.n_dp * self.n_fsdp
        assert self.count & (self.count - 1) == 0
        self.dp_index = lax.axis_index(DP)
        self.fsdp_index = lax.axis_index(FSDP)
        inner = []
        bit = 2
        while bit < self.n_dp:
            inner.append(bit)
            bit *= 2
        self.layout = ([1] if self.n_dp > 1 else []) + inner[::-1]

        self.sent, self.before = [], ()
        self.summed = []

    def swap(self, part, dp_bits, fsdp_bits=0):
        flip = dp_bits * self.n_fsdp + fsdp_bits
        return lax.ppermute(part, BOTH, [(i, i ^ flip) for i in range(self.count)])

    def queued(self, part, dp_bits, fsdp_bits=0):
        self.sent.append(Sent(self.swap(after(part, *self.before), dp_bits, fsdp_bits)))
        return self.sent[-1]

    def step(self, *ties):
        came = lax.optimization_barrier(tuple(one.value for one in self.sent))
        for one, value in zip(self.sent, came):
            one.value = value
        self.before, self.sent = came + ties, []

    def relative_blocks(self):
        found = [0]
        for bit in self.layout:
            found = [f + b for f in found for b in (0, bit)]
        return found


def after(value, *others):
    return lax.optimization_barrier((value,) + others)[0]


def turn_kernel(in_ref, out_ref):
    out_ref[...] = in_ref[...].T


def turned_block(block):
    rows, columns = block.shape
    return pl.pallas_call(
        turn_kernel,
        grid=(2,),
        in_specs=[pl.BlockSpec((rows, columns // 2), lambda i: (0, i))],
        out_specs=pl.BlockSpec((columns // 2, rows), lambda i: (i, 0)),
        out_shape=jax.ShapeDtypeStruct((columns, rows), block.dtype),
        compiler_params=params,
        cost_estimate=light,
    )(block)


class Gather:
    def __init__(self, grid, shard, turned=False):
        self.grid, self.shard, self.turned = grid, shard, turned
        self.line = None

    def direct_line(self):
        grid = self.grid
        self.pieces = [self.shard] + [grid.queued(self.shard, 0, k) for k in range(1, grid.n_fsdp)]

    def finish_line(self):
        if self.line is not None:
            return
        grid, pieces = self.grid, came(*self.pieces)
        bit = 1
        while bit < grid.n_fsdp:
            odd = (grid.fsdp_index & bit) != 0
            pieces = [jnp.where(odd, pieces[i ^ bit], pieces[i]) for i in range(grid.n_fsdp)]
            bit *= 2
        self.line = jnp.concatenate(pieces, axis=0)
        if self.turned:
            self.line = turned_block(self.line)

    def neighbours(self):
        self.finish_line()
        grid, block = self.grid, self.line
        inner = grid.layout[1:]
        self.pieces = [block]
        if len(inner) == 2:
            outer, near = inner
            self.pieces += [grid.queued(block, near), grid.queued(block, outer)]
        else:
            for bit in inner[::-1]:
                self.pieces = [jnp.concatenate(came(*self.pieces), axis=0)]
                self.pieces.append(grid.queued(self.pieces[0], bit))

    def opposite(self):
        grid = self.grid
        inner = grid.layout[1:]
        if len(inner) == 2:
            outer, near = inner
            middle = self.line.shape[0] // 32 * 16
            by_near, by_outer = came(*self.pieces[1:3])
            self.pieces += [
                grid.queued(by_near[:middle], outer),
                grid.queued(by_outer[middle:], near),
            ]

    def pair(self):
        self.own = jnp.concatenate(came(*self.pieces), axis=0)
        self.other = self.grid.queued(self.own, 1)

    def sides(self):
        return came(self.own, self.other)

    def by_block(self):
        sides = [side.reshape(-1, *self.line.shape) for side in self.sides()]
        if self.line.shape[1] % 128:
            sides = [jnp.concatenate(list(side), axis=1)[None] for side in sides]
        return tuple(sides)


def opposite_and_neighbours(one, two):
    grid = one.grid
    inner = grid.layout[1:]
    if len(inner) != 2:
        one.opposite()
        two.neighbours()
        return
    two.finish_line()
    outer, near = inner
    height = one.line.shape[0]
    middle = height // 32 * 16
    by_near, by_outer = came(*one.pieces[1:3])
    first = grid.queued(jnp.concatenate([by_near[:middle], two.line], axis=0), outer)
    second = grid.queued(jnp.concatenate([by_outer[middle:], two.line], axis=0), near)
    grid.step()
    one.pieces += [first.value[:middle], second.value[: height - middle]]
    two.pieces = [two.line, second.value[height - middle :], first.value[middle:]]


class Reduce:
    def __init__(self, grid, part, columns=False, turned=False):
        self.grid, self.part = grid, part
        self.met = self.sums = ()
        self.columns, self.turned = columns, turned

    def pair(self, *ties):
        self.high = self.part(1, ties=ties)
        self.arrived = self.grid.queued(self.high, 1)

    def opposite(self, *ties):
        grid = self.grid
        total = self.total = self.part(0, (self.arrived.value,), ties)
        if self.columns:
            width = D // grid.n_dp
            self.blocks = [total[:, i : i + width] for i in range(0, total.shape[1], width)]
        else:
            height = total.shape[0] // (grid.n_dp // 2)
            self.blocks = [total[i : i + height] for i in range(0, total.shape[0], height)]
        inner = grid.layout[1:]
        if len(inner) == 2:
            outer, near = inner
            self.middle = self.blocks[3].shape[0] // 32 * 16
            one, two = self.blocks[3][: self.middle], self.blocks[3][self.middle :]
            self.first, self.second = grid.queued(one, outer), grid.queued(two, near)
            self.met = tuple(came(self.first, self.second))

    def neighbours(self):
        grid = self.grid
        inner = grid.layout[1:]
        self.sums = []
        if len(inner) == 2:
            outer, near = inner
            rows, middle = self.blocks[0].shape[0], self.middle
            first, second = (part.astype(single) for part in self.met)
            to_near = self.blocks[1].astype(single) + jnp.pad(first, ((0, rows - middle), (0, 0)))
            to_outer = self.blocks[2].astype(single) + jnp.pad(second, ((middle, 0), (0, 0)))
            one, two = to_near.astype(bfloat), to_outer.astype(bfloat)
            self.sums = came(grid.queued(one, near), grid.queued(two, outer))
            total = self.blocks[0].astype(single)
            for part in self.sums:
                total = total + part.astype(single)
            self.block = total.astype(bfloat)
            return
        total = jnp.stack(self.blocks)
        for bit in inner:
            middle = total.shape[0] // 2
            away = grid.queued(total[middle:], bit).value
            total = (total[:middle].astype(single) + away.astype(single)).astype(bfloat)
        self.block = total[0]

    def along_line(self):
        block = self.block.T if self.turned else self.block
        summed = self.grid.summed
        if summed:
            block, summed[-1].shard = lax.optimization_barrier((block, summed[-1].shard))
        self.shard = lax.psum_scatter(block, FSDP, scatter_dimension=0, tiled=True)
        summed.append(self)

    def value(self):
        return self.shard.astype(single)


def total_everywhere(grid, part):
    bit = 1
    while bit < grid.n_dp:
        part = part + grid.swap(part, bit)
        bit *= 2
    bit = 1
    while bit < grid.n_fsdp:
        part = part + grid.swap(part, 0, bit)
        bit *= 2
    return part


def normalised(values):
    centred = values - jnp.mean(values, axis=-1, keepdims=True)
    spread = lax.rsqrt(jnp.mean(centred * centred, axis=-1, keepdims=True) + eps)
    return centred * spread, spread


def norm_gradient(grad, normal, spread, gain):
    scaled = grad * gain
    mean_one = jnp.mean(scaled, axis=-1, keepdims=True)
    mean_two = jnp.mean(scaled * normal, axis=-1, keepdims=True)
    return spread * (scaled - mean_one - normal * mean_two), jnp.sum(grad * normal, axis=0)


def gelu_exact(values):
    return jax.nn.gelu(values, approximate=False)


def positions(length, features):
    distances = jnp.arange(length, dtype=single)[::-1]
    freqs = jnp.exp(jnp.arange(features // 2, dtype=single) * (-2.0 * math.log(10000.0) / features))
    angles = distances[:, None] * freqs[None, :]
    return jnp.concatenate([jnp.sin(angles), jnp.cos(angles)], axis=1)


def lanes(*sides):
    return jnp.concatenate([side[i] for side in sides for i in range(side.shape[0])], axis=1)


def sums_of_experts(gates, blocks):
    return sum(gates[e : e + 1] * blocks[e * DH : (e + 1) * DH] for e in range(NE))


def each_expert(gates, block):
    return jnp.concatenate([gates[e : e + 1] * block for e in range(NE)], axis=0).astype(bfloat)


def expert_products(blocks, block):
    sums = [
        jnp.sum(blocks[e * DH : (e + 1) * DH].astype(single) * block, axis=0, keepdims=True)
        for e in range(NE)
    ]
    return jnp.concatenate(sums + [jnp.zeros_like(sums[0])] * (8 - NE), axis=0)


def mix_kernel(*refs):
    normed, rel, *sides = refs[:12]
    content_ref, position_ref, value_gate, output_gate = refs[12:16]
    qa_ref, qb_ref, k_ref, r_ref, v_ref, o_ref, p_ref, every_ref, gated_ref, out_ref = refs[16:]
    query, key, far, value, output = (lanes(*sides[i : i + 2]) for i in range(0, 10, 2))
    queries = dot(query, normed[MEM:, :], 1, 1)
    qa_ref[0] = (queries + content_ref[0]).astype(bfloat)
    qb_ref[0] = (queries + position_ref[0]).astype(bfloat)
    k_ref[0] = dot(key, normed[...], 1, 1).astype(bfloat)
    r_ref[0] = dot(far, rel[...], 1, 1).astype(bfloat)
    every = dot(value, normed[...], 1, 1)
    every_ref[0] = every.astype(bfloat)
    v_ref[0] = sums_of_experts(value_gate[0], every).astype(bfloat)
    bias = dot(qb_ref[0], r_ref[0], 0, 0)
    bias = pltpu.roll(bias, SPAN - SEG + 1, 1, stride=1, stride_axis=0)
    row = lax.broadcasted_iota(jnp.int32, (SEG, SPAN), 0)
    column = lax.broadcasted_iota(jnp.int32, (SEG, SPAN), 1)
    scores = (dot(qa_ref[0], k_ref[0], 0, 0) + bias) * scale
    scores = jnp.where(column <= MEM + row, scores, masked)
    powers = jnp.exp(scores - jnp.max(scores, axis=1, keepdims=True))
    weights = powers / jnp.sum(powers, axis=1, keepdims=True)
    p_ref[0] = weights
    attended = dot(v_ref[0], weights.astype(bfloat), 1, 1).astype(bfloat)
    o_ref[0] = attended
    gated = each_expert(output_gate[0], attended.astype(single))
    gated_ref[0] = gated

    @pl.when(pl.program_id(0) == 0)
    def _():
        out_ref[...] = jnp.zeros_like(out_ref)

    out_ref[...] += dot(gated, output, 0, 0)


def mix_back_kernel(*refs):
    grad_ref, *sides = refs[:9]
    qa_ref, qb_ref, k_ref, r_ref, v_ref, o_ref, p_ref, every_ref, value_gate, output_gate = refs[9:19]
    dq_ref, dk_ref, dr_ref, dv_ref, dzv_ref, dzo_ref, du_ref, dw_ref, out_ref = refs[-9:]
    query, key, value, output = (lanes(*sides[i : i + 2]) for i in range(0, 8, 2))
    back = dot(output, grad_ref[...], 1, 1)
    gate = output_gate[0]
    dzo_ref[0] = expert_products(back, o_ref[0].astype(single)) * gate * (1.0 - gate)
    grad_out = sums_of_experts(gate, back).astype(bfloat)
    weights = p_ref[0]
    grad_mixed = dot(grad_out, weights.astype(bfloat), 1, 0).astype(bfloat).astype(single)
    grad = dot(grad_out, v_ref[0], 0, 0).astype(bfloat).astype(single)
    grad = weights * (grad - jnp.sum(grad * weights, axis=1, keepdims=True)) * scale
    low = grad.astype(bfloat)
    grad_qa = dot(k_ref[0], low, 1, 1).astype(bfloat).astype(single)
    grad_key = dot(qa_ref[0], low, 1, 0).astype(bfloat)
    row = lax.broadcasted_iota(jnp.int32, (SEG, SEG), 0)
    column = lax.broadcasted_iota(jnp.int32, (SEG, SEG), 1)
    turn = jnp.where(row + column == SEG - 1, 1.0, 0.0).astype(bfloat)
    far = pltpu.roll(dot(turn, low, 1, 0), 0, 1, stride=1, stride_axis=0).astype(bfloat)
    dr_ref[0] = dot(dot(qb_ref[0], turn, 1, 0).astype(bfloat), far, 1, 0).astype(bfloat)
    grad_qb = dot(dot(r_ref[0], far, 1, 1).astype(bfloat), turn, 1, 0)
    du_ref[0] = jnp.sum(grad_qa, axis=1, keepdims=True)
    dw_ref[0] = jnp.sum(grad_qb, axis=1, keepdims=True)
    grad_query = (grad_qa + grad_qb).astype(bfloat)
    dq_ref[0, :, :MEM] = jnp.zeros((DH, MEM), bfloat)
    dq_ref[0, :, MEM:] = grad_query
    dk_ref[0] = grad_key
    gate = value_gate[0]
    dzv_ref[0] = expert_products(every_ref[0], grad_mixed) * gate * (1.0 - gate)
    grad_value = each_expert(gate, grad_mixed)
    dv_ref[0] = grad_value

    @pl.when(pl.program_id(0) == 0)
    def _():
        out_ref[...] = jnp.zeros_like(out_ref)

    out_ref[...] += dot(grad_key, key, 0, 0) + dot(grad_value, value, 0, 0)
    out_ref[MEM:, :] += dot(grad_query, query, 0, 0)


def head_rows(rows, columns, dtype=bfloat):
    block = pl.BlockSpec((1, rows, columns), lambda h: (h, 0, 0))
    return block, jax.ShapeDtypeStruct((H, rows, columns), dtype)


def weight_blocks(sides, start, rows):
    blocks, _, width = sides[0].shape
    return [pl.BlockSpec((blocks, rows, width), lambda h: (0, start // rows + h, 0))] * 2


def fixed(rows, columns):
    return pl.BlockSpec((rows, columns), lambda *_: (0, 0))


EXPERT = NE * DH


def mix(normed, rel, sides, content, position, value_gates, output_gates):
    outs = [
        head_rows(DH, SEG),
        head_rows(DH, SEG),
        head_rows(DH, SPAN),
        head_rows(DH, SPAN),
        head_rows(DH, SPAN),
        head_rows(DH, SEG),
        head_rows(SEG, SPAN, single),
        head_rows(EXPERT, SPAN),
        head_rows(EXPERT, SEG),
        (fixed(SEG, D), jax.ShapeDtypeStruct((SEG, D), single)),
    ]
    return pl.pallas_call(
        mix_kernel,
        grid=(H,),
        in_specs=[fixed(SPAN, D), fixed(SPAN, D)]
        + weight_blocks(sides, QUERY_ROW, DH)
        + weight_blocks(sides, QUERY_ROW + HD, DH)
        + weight_blocks(sides, POSITION_ROW, DH)
        + weight_blocks(sides, VALUE_ROW, EXPERT)
        + weight_blocks(sides, OUTPUT_ROW, EXPERT)
        + [head_rows(DH, 1)[0]] * 2
        + [head_rows(8, SPAN)[0], head_rows(8, SEG)[0]],
        out_specs=[spec for spec, _ in outs],
        out_shape=[shape for _, shape in outs],
        compiler_params=params,
        cost_estimate=light,
    )(normed, rel, *(sides * 5), content, position, value_gates, output_gates)


def mix_back(grad, sides, stored, value_gates, output_gates, ties):
    outs = [
        head_rows(DH, SPAN),
        head_rows(DH, SPAN),
        head_rows(DH, SPAN),
        head_rows(EXPERT, SPAN),
        head_rows(8, SPAN, single),
        head_rows(8, SEG, single),
        head_rows(DH, 1, single),
        head_rows(DH, 1, single),
        (fixed(SPAN, D), jax.ShapeDtypeStruct((SPAN, D), single)),
    ]
    return pl.pallas_call(
        mix_back_kernel,
        grid=(H,),
        in_specs=[fixed(SEG, D)]
        + weight_blocks(sides, QUERY_ROW, DH)
        + weight_blocks(sides, QUERY_ROW + HD, DH)
        + weight_blocks(sides, VALUE_ROW, EXPERT)
        + weight_blocks(sides, OUTPUT_ROW, EXPERT)
        + [head_rows(*array.shape[1:])[0] for array in stored]
        + [head_rows(8, SPAN)[0], head_rows(8, SEG)[0]]
        + [untouched] * len(ties),
        out_specs=[spec for spec, _ in outs],
        out_shape=[shape for _, shape in outs],
        compiler_params=params,
        cost_estimate=light,
    )(grad, *(sides * 4), *stored, value_gates, output_gates, *ties)


ff_tile = 1024
ff_columns = pl.BlockSpec((SEG, ff_tile), lambda i: (0, i))
ff_weights = pl.BlockSpec((D // 2, ff_tile), lambda i: (0, i))
ff_bias = pl.BlockSpec((1, ff_tile), lambda i: (0, i))


def expand_kernel(in_ref, own_ref, other_ref, bias_ref, act_ref, slope_ref):
    hidden = dot(in_ref[:, : D // 2], own_ref[...], 1, 0) + bias_ref[...]
    hidden = hidden + dot(in_ref[:, D // 2 :], other_ref[...], 1, 0)
    share = 0.5 + 0.5 * lax.erf(hidden * math.sqrt(0.5))
    act_ref[...] = (hidden * share).astype(bfloat)
    density = jnp.exp(hidden * hidden * -0.5) * (1.0 / math.sqrt(2.0 * math.pi))
    slope_ref[...] = (share + hidden * density).astype(bfloat)


def expand_forward(normed, sides, bias):
    wide = jax.ShapeDtypeStruct((SEG, FF), bfloat)
    return pl.pallas_call(
        expand_kernel,
        grid=(FF // ff_tile,),
        in_specs=[fixed(SEG, D), ff_weights, ff_weights, ff_bias],
        out_specs=[ff_columns, ff_columns],
        out_shape=[wide, wide],
        compiler_params=params,
        cost_estimate=light,
    )(normed, *sides, bias)


def contract_kernel(act_ref, own_ref, other_ref, out_ref):
    @pl.when(pl.program_id(0) == 0)
    def _():
        out_ref[...] = jnp.zeros_like(out_ref)

    out_ref[:, : D // 2] += dot(act_ref[...], own_ref[...], 1, 1)
    out_ref[:, D // 2 :] += dot(act_ref[...], other_ref[...], 1, 1)


def contract_forward(active, sides):
    return pl.pallas_call(
        contract_kernel,
        grid=(FF // ff_tile,),
        in_specs=[ff_columns, ff_weights, ff_weights],
        out_specs=fixed(SEG, D),
        out_shape=jax.ShapeDtypeStruct((SEG, D), single),
        compiler_params=params,
        cost_estimate=light,
    )(active, *sides)


def ff_back_kernel(in_ref, slope_ref, own_down, other_down, own_up, other_up, *refs):
    grad_ref, bias_ref, out_ref, total = refs[-4:]
    tile = pl.program_id(0)

    @pl.when(tile == 0)
    def _():
        total[...] = jnp.zeros_like(total)

    grad = dot(in_ref[:, : D // 2], own_down[...], 1, 0)
    grad = grad + dot(in_ref[:, D // 2 :], other_down[...], 1, 0)
    grad = grad.astype(bfloat).astype(single) * slope_ref[...].astype(single)
    low = grad.astype(bfloat)
    grad_ref[...] = low
    bias_ref[...] = jnp.sum(low.astype(single), axis=0, keepdims=True)
    total[:, : D // 2] += dot(low, own_up[...], 1, 1)
    total[:, D // 2 :] += dot(low, other_up[...], 1, 1)

    @pl.when(tile == pl.num_programs(0) - 1)
    def _():
        out_ref[...] = total[...].astype(bfloat)


def ff_back(grad, slope, down, up, ties):
    return pl.pallas_call(
        ff_back_kernel,
        grid=(FF // ff_tile,),
        in_specs=[fixed(SEG, D), ff_columns] + [ff_weights] * 4 + [untouched] * len(ties),
        out_specs=[ff_columns, ff_bias, fixed(SEG, D)],
        out_shape=[
            jax.ShapeDtypeStruct((SEG, FF), bfloat),
            jax.ShapeDtypeStruct((1, FF), single),
            jax.ShapeDtypeStruct((SEG, D), bfloat),
        ],
        scratch_shapes=[pltpu.VMEM((SEG, D), single)],
        compiler_params=params,
        cost_estimate=light,
    )(grad, slope, *down, *up, *ties)


untouched = pl.BlockSpec(memory_space=pl.ANY)


def product_kernel(left_dim, adds, left_ref, right_ref, *refs):
    total = dot(left_ref[...], right_ref[...], left_dim, 0)
    if adds:
        total = total + refs[0][...].astype(single)
    refs[-1][...] = total.astype(bfloat)


def ff_product(wide, other, side, came=(), ties=()):
    return pl.pallas_call(
        functools.partial(product_kernel, 0, len(came)),
        grid=(FF // ff_tile,),
        in_specs=[pl.BlockSpec((SEG, D // 2), lambda i: (0, side)), ff_columns]
        + [ff_weights] * len(came)
        + [untouched] * len(ties),
        out_specs=ff_weights,
        out_shape=jax.ShapeDtypeStruct((D // 2, FF), bfloat),
        compiler_params=params,
        cost_estimate=light,
    )(wide, other, *came, *ties)


def expert_product(wide, other, side, came=(), ties=()):
    rows, depth = other.shape
    tile = pl.BlockSpec((EXPERT, D // 2), lambda i: (i, 0))
    return pl.pallas_call(
        functools.partial(product_kernel, 1, len(came)),
        grid=(rows // EXPERT,),
        in_specs=[
            pl.BlockSpec((EXPERT, depth), lambda i: (i, 0)),
            pl.BlockSpec((depth, D // 2), lambda i: (0, side)),
        ]
        + [tile] * len(came)
        + [untouched] * len(ties),
        out_specs=tile,
        out_shape=jax.ShapeDtypeStruct((rows, D // 2), bfloat),
        compiler_params=params,
        cost_estimate=light,
    )(other, wide, *came, *ties)


def table_product_kernel(first, adds, grad_ref, ids_ref, out_grad, in_grad, *refs):
    rows = grad_ref.shape[1]
    place = first + pl.program_id(0) * rows + lax.broadcasted_iota(jnp.int32, (rows, SEG), 0)
    chosen = jnp.where(place == ids_ref[...], 1.0, 0.0).astype(bfloat)
    total = dot(grad_ref[...], out_grad[...], 0, 0) + dot(chosen, in_grad[...], 1, 0)
    if adds:
        total = total + refs[0][...].astype(single)
    refs[-1][...] = total.astype(bfloat)


def table_product(grad_logits, ids, normed, grad_embedded, first, rows, side, came=(), ties=()):
    half = pl.BlockSpec((SEG, D // 2), lambda i: (0, side))
    tile = pl.BlockSpec((head_tile, D // 2), lambda i: (i, 0))
    return pl.pallas_call(
        functools.partial(table_product_kernel, first, len(came)),
        grid=(rows // head_tile,),
        in_specs=[
            pl.BlockSpec((SEG, head_tile), lambda i: (0, first // head_tile + i)),
            fixed(1, SEG),
            half,
            half,
        ]
        + [tile] * len(came)
        + [untouched] * len(ties),
        out_specs=tile,
        out_shape=jax.ShapeDtypeStruct((rows, D // 2), bfloat),
        compiler_params=params,
        cost_estimate=light,
    )(grad_logits, ids, normed, grad_embedded, *came, *ties)


def small_product_kernel(adds, q_ref, k_ref, r_ref, gates_ref, vectors_ref, normed, rel, *refs):
    out = refs[-1]

    def put(start, value):
        stop = start + value.shape[0]
        if adds:
            value = value + refs[0][start:stop, :].astype(single)
        out[start:stop, :] = value.astype(bfloat)

    put(0, dot(q_ref[...], normed[...], 1, 0))
    put(HD, dot(k_ref[...], normed[...], 1, 0))
    put(2 * HD, dot(r_ref[...], rel[...], 1, 0))
    put(3 * HD, dot(gates_ref[...], normed[...], 1, 0) + vectors_ref[...])


def small_product(grads, vectors, normed, rel, side, came=(), ties=()):
    def half(rows):
        return pl.BlockSpec((rows, D // 2), lambda i: (0, side))

    rows = 3 * HD + LAST_ROWS
    return pl.pallas_call(
        functools.partial(small_product_kernel, len(came)),
        grid=(1,),
        in_specs=[fixed(*grad.shape) for grad in grads]
        + [half(LAST_ROWS), half(SPAN), half(SPAN)]
        + [fixed(rows, D // 2)] * len(came)
        + [untouched] * len(ties),
        out_specs=fixed(rows, D // 2),
        out_shape=jax.ShapeDtypeStruct((rows, D // 2), bfloat),
        compiler_params=params,
        cost_estimate=light,
    )(*grads, vectors, normed, rel, *came, *ties)


def lookup_kernel(first, ids_ref, own_ref, other_ref, out_ref):
    tile = pl.program_id(0)
    rows = own_ref.shape[1]
    place = first + tile * rows + lax.broadcasted_iota(jnp.int32, (SEG, rows), 1)
    chosen = jnp.where(ids_ref[...] == place, 1.0, 0.0).astype(bfloat)
    found = dot(chosen, lanes(own_ref, other_ref), 1, 0)

    @pl.when(tile == 0)
    def _():
        out_ref[...] = found

    @pl.when(tile > 0)
    def _():
        out_ref[...] += found


def lookup(ids, own, other, first):
    blocks, rows, width = own.shape
    tile = 1024
    side = pl.BlockSpec((blocks, tile, width), lambda i: (0, i, 0))
    return pl.pallas_call(
        functools.partial(lookup_kernel, first),
        grid=(rows // tile,),
        in_specs=[pl.BlockSpec((SEG, 1), lambda i: (0, 0)), side, side],
        out_specs=pl.BlockSpec((SEG, D), lambda i: (0, 0)),
        out_shape=jax.ShapeDtypeStruct((SEG, D), single),
        compiler_params=params,
        cost_estimate=light,
    )(ids, own, other)


head_tile = 512


def head_kernel(
    shard_rows,
    shard_half,
    hf_ref,
    goal_ref,
    counted_ref,
    own_zero,
    other_zero,
    own_one,
    other_one,
    grad_ref,
    back_ref,
    loss_ref,
    logits,
    total,
    highest,
    summed,
    picked,
):
    tiles = pl.num_programs(0) // 2
    step = pl.program_id(0)
    tile = lax.rem(step, tiles)
    at = pl.multiple_of(tile * head_tile, head_tile)
    place = at + lax.broadcasted_iota(jnp.int32, (SEG, head_tile), 1)
    hits = place == goal_ref[...]

    def each_table(use):
        @pl.when(tile < tiles // 2)
        def _():
            use(lanes(own_zero, other_zero), 0)

        @pl.when(tile >= tiles // 2)
        def _():
            use(lanes(own_one, other_one), shard_half)

    def groups(values):
        return [values[:, i : i + 128] for i in range(0, head_tile, 128)]

    @pl.when(step == 0)
    def _():
        highest[...] = jnp.full_like(highest, masked)
        summed[...] = jnp.zeros_like(summed)
        picked[...] = jnp.zeros_like(picked)
        total[...] = jnp.zeros_like(total)

    @pl.when(step < tiles)
    def _():
        def use(rows, late):
            scores = dot(hf_ref[...], rows, 1, 1)
            scores = jnp.where(lax.rem(place, shard_half) + late < shard_rows, scores, masked)
            logits[:, pl.ds(at, head_tile)] = scores
            parts = groups(scores)
            top = functools.reduce(jnp.maximum, parts, highest[...])
            powers = sum(jnp.exp(part - top) for part in parts)
            summed[...] = summed[...] * jnp.exp(highest[...] - top) + powers
            highest[...] = top
            picked[...] += sum(groups(jnp.where(hits, scores, 0.0)))

        each_table(use)

    @pl.when(step == tiles)
    def _():
        top = jnp.max(highest[...], axis=1, keepdims=True)
        powers = jnp.sum(summed[...] * jnp.exp(highest[...] - top), axis=1, keepdims=True)
        whole = top + jnp.log(powers)
        loss_ref[...] = (whole - jnp.sum(picked[...], axis=1, keepdims=True)) * counted_ref[...]
        highest[...] = jnp.broadcast_to(whole, highest.shape)

    @pl.when(step >= tiles)
    def _():
        def use(rows, late):
            shares = jnp.exp(logits[:, pl.ds(at, head_tile)] - highest[:, :1])
            grad = ((shares - jnp.where(hits, 1.0, 0.0)) * counted_ref[...]).astype(bfloat)
            grad_ref[...] = grad
            total[...] += dot(grad, rows, 1, 0)

        each_table(use)

    @pl.when(step == 2 * tiles - 1)
    def _():
        back_ref[...] = total[...].astype(bfloat)


def head(hf, goals, counted, parts, shard_rows, shard_half):
    blocks, rows, width = parts[0][0].shape
    half_tiles = rows // head_tile
    tiles = 2 * half_tiles

    def side(part):
        def index(i):
            return 0, jnp.clip(lax.rem(i, tiles) - part * half_tiles, 0, half_tiles - 1), 0

        return pl.BlockSpec((blocks, head_tile, width), index)

    column = pl.BlockSpec((SEG, 1), lambda i: (0, 0))
    whole = pl.BlockSpec((SEG, D), lambda i: (0, 0))
    return pl.pallas_call(
        functools.partial(head_kernel, shard_rows, shard_half),
        grid=(2 * tiles,),
        in_specs=[whole, column, column, side(0), side(0), side(1), side(1)],
        out_specs=[
            pl.BlockSpec((SEG, head_tile), lambda i: (0, jnp.maximum(i - tiles, 0))),
            whole,
            column,
        ],
        out_shape=[
            jax.ShapeDtypeStruct((SEG, 2 * rows), bfloat),
            jax.ShapeDtypeStruct((SEG, D), bfloat),
            jax.ShapeDtypeStruct((SEG, 1), single),
        ],
        scratch_shapes=[
            pltpu.VMEM((SEG, 2 * rows), single),
            pltpu.VMEM((SEG, D), single),
            pltpu.VMEM((SEG, 128), single),
            pltpu.VMEM((SEG, 128), single),
            pltpu.VMEM((SEG, 128), single),
        ],
        compiler_params=params,
        cost_estimate=light,
    )(hf, goals, counted, *parts[0], *parts[1])


def chosen_experts(routes, slots, capacity):
    experts = jnp.arange(NE, dtype=jnp.int32)[None, :, None, None]
    turned = jnp.transpose(routes, (1, 2, 0))[:, None]
    kept = jnp.transpose(slots, (1, 2, 0))[:, None] < capacity
    return jnp.sum(((turned == experts) & kept).astype(single), axis=2)


def advance(weight, velocity, average, grad, factor, step_rate):
    clipped = grad * factor
    velocity_next = momentum_decay * velocity + clipped
    updated = weight - step_rate * (clipped + momentum_decay * velocity_next)
    return (velocity_next, updated, average + (updated - average) / (STEP + 1))


def table_shape(grid):
    rows = V // grid.n_fsdp
    return rows, -(-rows // 256) * 128


def table_place(grid, ids):
    rows, part = table_shape(grid)
    owner, row = ids // rows, ids % rows
    return (row // part) * (grid.n_fsdp * part) + owner * part + row % part


def body(
    token_ids,
    targets,
    target_counts,
    memory,
    value_routes,
    value_slots,
    output_routes,
    output_slots,
    *states,
):
    masters, moments, averages = states[0::3], states[1::3], states[2::3]
    embedding, projector, position, values, outputs, expand, contract, vectors, biases = masters
    grid = Grid()
    ids = table_place(grid, token_ids[0])
    goals = table_place(grid, targets[0])
    half = D // 2
    chunk = D // grid.count

    shard_rows, shard_half = table_shape(grid)
    part_rows = shard_half * grid.n_fsdp
    table_shard = jnp.pad(embedding.astype(bfloat), ((0, 2 * shard_half - shard_rows), (0, 0)))
    expanding = Gather(grid, expand.astype(bfloat))
    contracting = Gather(grid, contract.T.astype(bfloat))
    tables = [Gather(grid, table_shard[i : i + shard_half]) for i in (0, shard_half)]
    attention_shard = jnp.concatenate(
        [
            values.astype(bfloat),
            outputs.T.astype(bfloat),
            projector[:, :QUERIES].astype(bfloat),
            position.astype(bfloat),
            projector[:, QUERIES:].astype(bfloat),
            vectors.T.astype(bfloat),
            jnp.zeros((chunk, LAST_ROWS - GATES - 4), bfloat),
        ],
        axis=1,
    )
    attending = Gather(grid, attention_shard, True)
    distances = jnp.array(grid.relative_blocks(), jnp.int32)
    width = D // grid.n_dp
    true_columns = (
        (distances[:, None] ^ grid.dp_index) * width + jnp.arange(width, dtype=jnp.int32)[None, :]
    ).reshape(D)
    to_order = (jnp.arange(D, dtype=jnp.int32)[:, None] == true_columns[None, :]).astype(bfloat)
    memory_rows = dot(memory[0], to_order, 1, 0)
    rel_table = dot(positions(SPAN, D).astype(bfloat), to_order, 1, 0).astype(bfloat)

    tables[0].direct_line()
    grid.step(memory_rows, rel_table)
    tables[0].neighbours()
    tables[1].direct_line()
    grid.step()
    attending.direct_line()
    opposite_and_neighbours(tables[0], tables[1])
    middle = expand.shape[1]
    lines = lax.all_gather(
        after(jnp.concatenate([expanding.shard, contracting.shard], axis=1), *grid.before),
        FSDP,
        axis=0,
        tiled=True,
    )
    expanding.line, contracting.line = lines[:, :middle], lines[:, middle:]
    tables[1].opposite()
    tables[0].pair()
    attending.neighbours()
    grid.step()
    attending.opposite()
    expanding.neighbours()
    tables[1].pair()
    found = [lookup(ids[:, None], *tables[0].by_block(), 0)]
    grid.step(found[0])
    tables_by_block = [part.by_block() for part in tables]
    attending.pair()
    expanding.opposite()
    found.append(lookup(ids[:, None], *tables_by_block[1], part_rows))
    embedded = (found[0] + found[1]) * D**0.5
    grid.step(embedded)
    contracting.neighbours()
    expanding.pair()
    attention = attending.by_block()
    last_rows = jnp.concatenate(
        [side[i, GATE_ROW:] for side in attention for i in range(side.shape[0])], axis=1
    )
    gains = last_rows[GATES : GATES + 4].astype(single)

    stream = jnp.concatenate([memory_rows, embedded], axis=0)
    normal_in, spread_in = normalised(stream)
    normed = (normal_in * gains[0]).astype(bfloat)
    logits = jax.nn.sigmoid(dot(last_rows, normed, 1, 1)[:GATES])

    def gates_of(shares, routes, slots, capacity):
        kept = shares.reshape(H, NE, -1) * chosen_experts(routes, slots, capacity)
        return jnp.pad(kept, ((0, 0), (0, 8 - NE), (0, 0)))

    value_gates = gates_of(logits[: H * NE], value_routes[0], value_slots[0], CAPV)
    output_gates = gates_of(logits[H * NE :, MEM:], output_routes[0], output_slots[0], CAPO)
    *stored, gated, mixed = mix(
        normed,
        rel_table,
        attention,
        biases[:HD].reshape(H, DH, 1),
        biases[HD : 2 * HD].reshape(H, DH, 1),
        value_gates,
        output_gates,
    )
    grid.step(mixed)
    contracting.opposite()
    gated = gated.reshape(H * EXPERT, SEG)
    residual = embedded + mixed
    normal_mid, spread_mid = normalised(residual)
    normed_mid = (normal_mid * gains[1]).astype(bfloat)
    up = expanding.sides()
    active, slope = expand_forward(normed_mid, up, biases[None, 2 * HD :])
    grid.step()
    contracting.pair()
    grid.step()
    down = contracting.sides()
    final = residual + contract_forward(active, down) + gains[3]
    normal_out, spread_out = normalised(final)
    normed_out = (normal_out * gains[2]).astype(bfloat)

    counted = (jnp.arange(SEG, dtype=jnp.int32) < target_counts[0]).astype(single)
    grad_logits, grad_out, losses = head(
        normed_out, goals[:, None], counted[:, None], tables_by_block, shard_rows, shard_half
    )
    loss = jnp.sum(losses)

    grad_final, grad_gain_out = norm_gradient(
        grad_out.astype(single), normal_out, spread_out, gains[2]
    )
    grad_branch = grad_final.astype(bfloat)
    grad_bias_down = jnp.sum(grad_branch.astype(single), axis=0)

    def summing(wide, other):
        return Reduce(grid, functools.partial(ff_product, wide, other))

    def summing_turned(wide, other):
        return Reduce(grid, functools.partial(expert_product, wide, other), True, True)

    grid.step()
    contracting = summing(grad_branch, active)
    contracting.pair()
    grad_hidden, grad_bias_up, grad_mid = ff_back(
        grad_branch, slope, down, up, [contracting.high]
    )
    expanding = summing(normed_mid, grad_hidden)
    expanding.pair()
    contracting.opposite(expanding.high)
    expanding.opposite(contracting.total)
    grad_residual, grad_gain_mid = norm_gradient(
        grad_mid.astype(single), normal_mid, spread_mid, gains[1]
    )
    grad_residual = grad_residual + grad_final
    low_residual = grad_residual.astype(bfloat)
    outputting = summing_turned(low_residual, gated)
    outputting.pair(expanding.total)
    contracting.neighbours()
    expanding.neighbours()
    (
        grad_queries,
        grad_keys,
        grad_rel,
        grad_values,
        grad_value_gates,
        grad_output_gates,
        grad_content,
        grad_position,
        grad_normed,
    ) = mix_back(
        low_residual,
        attention,
        stored,
        value_gates,
        output_gates,
        [outputting.high, *contracting.met, *expanding.met],
    )
    grad_values = grad_values.reshape(H * EXPERT, SPAN)
    valuing = summing_turned(normed, grad_values)
    valuing.pair(*contracting.sums)
    outputting.opposite(valuing.high)
    grad_gates = jnp.concatenate(
        [
            grad_value_gates[:, :NE].reshape(H * NE, SPAN),
            jnp.pad(grad_output_gates[:, :NE].reshape(H * NE, SEG), ((0, 0), (MEM, 0))),
            jnp.zeros((LAST_ROWS - GATES, SPAN), single),
        ],
        axis=0,
    ).astype(bfloat)
    contracting.along_line()
    grad_normed = (grad_normed + dot(grad_gates, last_rows, 0, 0)).astype(bfloat)
    grad_stream, grad_gain_in = norm_gradient(
        grad_normed.astype(single), normal_in, spread_in, gains[0]
    )
    grad_embedded = (grad_residual + grad_stream[MEM:]).astype(bfloat)
    nothing = jnp.zeros((D,), single)
    grad_vectors = jnp.stack(
        [nothing] * GATES
        + [grad_gain_in, grad_gain_mid, grad_gain_out, grad_bias_down]
        + [nothing] * (LAST_ROWS - GATES - 4)
    )

    def table_summing(first):
        part = functools.partial(
            table_product,
            grad_logits,
            ids[None, :],
            normed_out,
            grad_embedded * bfloat(D**0.5),
            first,
            part_rows,
        )
        return Reduce(grid, part, True)

    tables = [table_summing(i) for i in (0, part_rows)]
    grads = [part.reshape(HD, SPAN) for part in (grad_queries, grad_keys, grad_rel)] + [grad_gates]
    small = functools.partial(small_product, grads, grad_vectors, normed, rel_table)
    smalling = Reduce(grid, small, True, True)
    expanding.along_line()
    outputting.neighbours()
    tables[0].pair(outputting.total, *expanding.sums)
    smalling.pair(tables[0].high)
    valuing.opposite(smalling.high, *outputting.met)
    outputting.along_line()
    tables[1].pair(valuing.total, contracting.shard)
    smalling.opposite(tables[1].high)
    valuing.neighbours()
    tables[0].opposite(smalling.total, *valuing.met, *outputting.sums)
    smalling.neighbours()
    tables[1].opposite(tables[0].total, *valuing.sums, *smalling.met)
    tables[0].neighbours()
    tables[1].neighbours()
    for part in (valuing, smalling, tables[0], tables[1]):
        part.along_line()
    sum_contract, sum_expand, sum_outputs, sum_values, sum_small = (
        part.value() for part in (contracting, expanding, outputting, valuing, smalling)
    )
    sum_table = jnp.concatenate([part.value() for part in tables], axis=0)[:shard_rows]

    shard_grads = [
        sum_table,
        jnp.concatenate([sum_small[:, :QUERIES], sum_small[:, 3 * HD : 3 * HD + GATES]], axis=1),
        sum_small[:, QUERIES : 3 * HD],
        sum_values,
        sum_outputs.T,
        sum_expand,
        sum_contract.T,
        sum_small[:, 3 * HD + GATES : 3 * HD + GATES + 4].T,
    ]
    most_tokens = grid.count * SEG
    local_squares = jnp.zeros((), single)
    for part in tables + [contracting, expanding, outputting, valuing, smalling]:
        scaled = part.value() * (1.0 / most_tokens)
        local_squares = local_squares + jnp.sum(scaled * scaled)
    shared = jnp.concatenate(
        [
            grad_content.reshape(HD),
            grad_position.reshape(HD),
            grad_bias_up.reshape(FF),
            jnp.stack([loss, target_counts[0].astype(single), local_squares]),
        ]
    )
    shared = total_everywhere(grid, shared)
    bias_grad, loss_total, token_count, squares = shared[:-3], shared[-3], shared[-2], shared[-1]
    scaled = bias_grad * (1.0 / most_tokens)
    gradient_norm = jnp.sqrt(squares + jnp.sum(scaled * scaled)) * (most_tokens / token_count)
    factor = jnp.minimum(1.0, clip_norm / (gradient_norm + 1e-06))
    inverse = 1.0 / token_count
    shard_grads = [grad * inverse for grad in shard_grads]
    bias_grad = bias_grad * inverse
    step_rate = rate_base * (PARAMS / D) ** 0.5
    results = (loss_total, token_count, gradient_norm)
    for weight, velocity, average, grad, multiplier in zip(
        masters, moments, averages, shard_grads + [bias_grad], rate_factors
    ):
        results += advance(weight, velocity, average, grad, factor, step_rate * multiplier)
    return results


def solution(mesh):
    batch = P(BOTH)
    rows, columns, whole = P(BOTH, None), P(None, BOTH), P()
    kinds = (P(FSDP, DP), rows, rows, rows, columns, rows, columns, columns, whole)
    triples = tuple(kind for kind in kinds for _ in range(3))
    return jax.shard_map(
        body,
        mesh=mesh,
        in_specs=(batch,) * 8 + triples,
        out_specs=(whole,) * 3 + triples,
        check_vma=False,
    )
```

```python
import functools
import math

import jax
import jax.numpy as jnp
from jax import lax
from jax.experimental import pallas as pl
from jax.experimental.pallas import tpu as pltpu
from jax.sharding import PartitionSpec as P

D = 1024
H = 4
DH = 112
NE = 5
FF = 4096
V = 8000
SEG = 512
MEM = 512
STEP = 8
SPAN = 1024
CAPV = 512
CAPO = 256
HD = H * DH
QUERIES = 2 * HD
VALUE_ROW = 0
OUTPUT_ROW = 2240
QUERY_ROW = 4480
POSITION_ROW = 5376
GATE_ROW = 5824
GATES = 2 * H * NE
LAST_ROWS = 64
PARAMS = 22594432

eps = 1e-05
clip_norm = 0.02
momentum_decay = 0.9
rate_base = 10.0
rate_factors = (1.0, 1.0, 1.0, 1.0, 500.0, 1.0, 1.0, 1.0, 8.0)
masked = -1e30
scale = DH ** (-0.5)
bfloat = jnp.bfloat16
single = jnp.float32
DP, FSDP = "dp", "fsdp"
BOTH = (DP, FSDP)
vmem_bytes = 56 * 1024 * 1024
params = pltpu.CompilerParams(vmem_limit_bytes=vmem_bytes)
light = pl.CostEstimate(flops=10**7, bytes_accessed=10**5, transcendentals=0)


def dot(left, right, left_dim, right_dim):
    return lax.dot_general(
        left, right, (((left_dim,), (right_dim,)), ((), ())), preferred_element_type=single
    )


class Sent:
    def __init__(self, value):
        self.value = value


def came(*parts):
    return [part.value if isinstance(part, Sent) else part for part in parts]


class Grid:
    def __init__(self):
        self.n_dp = lax.axis_size(DP)
        self.n_fsdp = lax.axis_size(FSDP)
        self.count = self.n_dp * self.n_fsdp
        assert self.count & (self.count - 1) == 0
        self.dp_index = lax.axis_index(DP)
        self.fsdp_index = lax.axis_index(FSDP)
        inner = []
        bit = 2
        while bit < self.n_dp:
            inner.append(bit)
            bit *= 2
        self.layout = ([1] if self.n_dp > 1 else []) + inner[::-1]

        self.sent, self.before = [], ()
        self.summed = []

    def swap(self, part, dp_bits, fsdp_bits=0):
        flip = dp_bits * self.n_fsdp + fsdp_bits
        return lax.ppermute(part, BOTH, [(i, i ^ flip) for i in range(self.count)])

    def queued(self, part, dp_bits, fsdp_bits=0):
        self.sent.append(Sent(self.swap(after(part, *self.before), dp_bits, fsdp_bits)))
        return self.sent[-1]

    def step(self, *ties):
        came = lax.optimization_barrier(tuple(one.value for one in self.sent))
        for one, value in zip(self.sent, came):
            one.value = value
        self.before, self.sent = came + ties, []

    def relative_blocks(self):
        found = [0]
        for bit in self.layout:
            found = [f + b for f in found for b in (0, bit)]
        return found


def after(value, *others):
    return lax.optimization_barrier((value,) + others)[0]


def turn_kernel(in_ref, out_ref):
    out_ref[...] = in_ref[...].T


def turned_block(block):
    rows, columns = block.shape
    return pl.pallas_call(
        turn_kernel,
        grid=(2,),
        in_specs=[pl.BlockSpec((rows, columns // 2), lambda i: (0, i))],
        out_specs=pl.BlockSpec((columns // 2, rows), lambda i: (i, 0)),
        out_shape=jax.ShapeDtypeStruct((columns, rows), block.dtype),
        compiler_params=params,
        cost_estimate=light,
    )(block)


class Gather:
    def __init__(self, grid, shard, turned=False):
        self.grid, self.shard, self.turned = grid, shard, turned
        self.line = None

    def direct_line(self):
        grid = self.grid
        self.pieces = [self.shard] + [grid.queued(self.shard, 0, k) for k in range(1, grid.n_fsdp)]

    def finish_line(self):
        if self.line is not None:
            return
        grid, pieces = self.grid, came(*self.pieces)
        bit = 1
        while bit < grid.n_fsdp:
            odd = (grid.fsdp_index & bit) != 0
            pieces = [jnp.where(odd, pieces[i ^ bit], pieces[i]) for i in range(grid.n_fsdp)]
            bit *= 2
        self.line = jnp.concatenate(pieces, axis=0)
        if self.turned:
            self.line = turned_block(self.line)

    def neighbours(self):
        self.finish_line()
        grid, block = self.grid, self.line
        inner = grid.layout[1:]
        self.pieces = [block]
        if len(inner) == 2:
            outer, near = inner
            self.pieces += [grid.queued(block, near), grid.queued(block, outer)]
        else:
            for bit in inner[::-1]:
                self.pieces = [jnp.concatenate(came(*self.pieces), axis=0)]
                self.pieces.append(grid.queued(self.pieces[0], bit))

    def opposite(self):
        grid = self.grid
        inner = grid.layout[1:]
        if len(inner) == 2:
            outer, near = inner
            middle = self.line.shape[0] // 32 * 16
            by_near, by_outer = came(*self.pieces[1:3])
            self.pieces += [
                grid.queued(by_near[:middle], outer),
                grid.queued(by_outer[middle:], near),
            ]

    def pair(self):
        self.own = jnp.concatenate(came(*self.pieces), axis=0)
        self.other = self.grid.queued(self.own, 1)

    def sides(self):
        return came(self.own, self.other)

    def by_block(self):
        sides = [side.reshape(-1, *self.line.shape) for side in self.sides()]
        if self.line.shape[1] % 128:
            sides = [jnp.concatenate(list(side), axis=1)[None] for side in sides]
        return tuple(sides)


def opposite_and_neighbours(one, two):
    grid = one.grid
    inner = grid.layout[1:]
    if len(inner) != 2:
        one.opposite()
        two.neighbours()
        return
    two.finish_line()
    outer, near = inner
    height = one.line.shape[0]
    middle = height // 32 * 16
    by_near, by_outer = came(*one.pieces[1:3])
    first = grid.queued(jnp.concatenate([by_near[:middle], two.line], axis=0), outer)
    second = grid.queued(jnp.concatenate([by_outer[middle:], two.line], axis=0), near)
    grid.step()
    one.pieces += [first.value[:middle], second.value[: height - middle]]
    two.pieces = [two.line, second.value[height - middle :], first.value[middle:]]


class Reduce:
    def __init__(self, grid, part, columns=False, turned=False):
        self.grid, self.part = grid, part
        self.met = self.sums = self.away = ()
        self.columns, self.turned = columns, turned

    def pair(self, *ties):
        self.high = self.part(1, ties=ties)
        self.arrived = self.grid.queued(self.high, 1)

    def opposite(self, *ties):
        grid = self.grid
        total = self.total = self.part(0, (self.arrived.value,), ties)
        if self.columns:
            width = D // grid.n_dp
            self.blocks = [total[:, i : i + width] for i in range(0, total.shape[1], width)]
        else:
            height = total.shape[0] // (grid.n_dp // 2)
            self.blocks = [total[i : i + height] for i in range(0, total.shape[0], height)]
        inner = grid.layout[1:]
        if len(inner) == 2:
            outer, near = inner
            self.middle = self.blocks[3].shape[0] // 32 * 16
            one, two = self.blocks[3][: self.middle], self.blocks[3][self.middle :]
            self.first, self.second = grid.queued(one, outer), grid.queued(two, near)
            self.met = tuple(came(self.first, self.second))

    def neighbours(self):
        grid = self.grid
        inner = grid.layout[1:]
        self.sums = []
        if len(inner) == 2:
            outer, near = inner
            rows, middle = self.blocks[0].shape[0], self.middle
            first, second = (part.astype(single) for part in self.met)
            to_near = self.blocks[1].astype(single) + jnp.pad(first, ((0, rows - middle), (0, 0)))
            to_outer = self.blocks[2].astype(single) + jnp.pad(second, ((middle, 0), (0, 0)))
            one, two = self.away = (to_near.astype(bfloat), to_outer.astype(bfloat))
            self.sums = came(grid.queued(one, near), grid.queued(two, outer))
            total = self.blocks[0].astype(single)
            for part in self.sums:
                total = total + part.astype(single)
            self.block = total.astype(bfloat)
            return
        total = jnp.stack(self.blocks)
        for bit in inner:
            middle = total.shape[0] // 2
            away = grid.queued(total[middle:], bit).value
            total = (total[:middle].astype(single) + away.astype(single)).astype(bfloat)
        self.block = total[0]

    def along_line(self):
        block = self.block.T if self.turned else self.block
        summed = self.grid.summed
        if summed:
            block, summed[-1].shard = lax.optimization_barrier((block, summed[-1].shard))
        self.shard = lax.psum_scatter(block, FSDP, scatter_dimension=0, tiled=True)
        summed.append(self)

    def value(self):
        return self.shard.astype(single)


def total_everywhere(grid, part):
    bit = 1
    while bit < grid.n_dp:
        part = part + grid.swap(part, bit)
        bit *= 2
    bit = 1
    while bit < grid.n_fsdp:
        part = part + grid.swap(part, 0, bit)
        bit *= 2
    return part


def normalised(values):
    centred = values - jnp.mean(values, axis=-1, keepdims=True)
    spread = lax.rsqrt(jnp.mean(centred * centred, axis=-1, keepdims=True) + eps)
    return centred * spread, spread


def norm_gradient(grad, normal, spread, gain):
    scaled = grad * gain
    mean_one = jnp.mean(scaled, axis=-1, keepdims=True)
    mean_two = jnp.mean(scaled * normal, axis=-1, keepdims=True)
    return spread * (scaled - mean_one - normal * mean_two), jnp.sum(grad * normal, axis=0)


def gelu_exact(values):
    return jax.nn.gelu(values, approximate=False)


def positions(length, features):
    distances = jnp.arange(length, dtype=single)[::-1]
    freqs = jnp.exp(jnp.arange(features // 2, dtype=single) * (-2.0 * math.log(10000.0) / features))
    angles = distances[:, None] * freqs[None, :]
    return jnp.concatenate([jnp.sin(angles), jnp.cos(angles)], axis=1)


def lanes(*sides):
    return jnp.concatenate([side[i] for side in sides for i in range(side.shape[0])], axis=1)


def sums_of_experts(gates, blocks):
    return sum(gates[e : e + 1] * blocks[e * DH : (e + 1) * DH] for e in range(NE))


def each_expert(gates, block):
    return jnp.concatenate([gates[e : e + 1] * block for e in range(NE)], axis=0).astype(bfloat)


def expert_products(blocks, block):
    sums = [
        jnp.sum(blocks[e * DH : (e + 1) * DH].astype(single) * block, axis=0, keepdims=True)
        for e in range(NE)
    ]
    return jnp.concatenate(sums + [jnp.zeros_like(sums[0])] * (8 - NE), axis=0)


def mix_kernel(*refs):
    normed, rel, *sides = refs[:12]
    content_ref, position_ref, value_gate, output_gate = refs[12:16]
    qa_ref, qb_ref, k_ref, r_ref, v_ref, o_ref, p_ref, every_ref, gated_ref, out_ref = refs[16:]
    query, key, far, value, output = (lanes(*sides[i : i + 2]) for i in range(0, 10, 2))
    queries = dot(query, normed[MEM:, :], 1, 1)
    qa_ref[0] = (queries + content_ref[0]).astype(bfloat)
    qb_ref[0] = (queries + position_ref[0]).astype(bfloat)
    k_ref[0] = dot(key, normed[...], 1, 1).astype(bfloat)
    r_ref[0] = dot(far, rel[...], 1, 1).astype(bfloat)
    every = dot(value, normed[...], 1, 1)
    every_ref[0] = every.astype(bfloat)
    v_ref[0] = sums_of_experts(value_gate[0], every).astype(bfloat)
    bias = dot(qb_ref[0], r_ref[0], 0, 0)
    bias = pltpu.roll(bias, SPAN - SEG + 1, 1, stride=1, stride_axis=0)
    row = lax.broadcasted_iota(jnp.int32, (SEG, SPAN), 0)
    column = lax.broadcasted_iota(jnp.int32, (SEG, SPAN), 1)
    scores = (dot(qa_ref[0], k_ref[0], 0, 0) + bias) * scale
    scores = jnp.where(column <= MEM + row, scores, masked)
    powers = jnp.exp(scores - jnp.max(scores, axis=1, keepdims=True))
    weights = powers / jnp.sum(powers, axis=1, keepdims=True)
    p_ref[0] = weights
    attended = dot(v_ref[0], weights.astype(bfloat), 1, 1).astype(bfloat)
    o_ref[0] = attended
    gated = each_expert(output_gate[0], attended.astype(single))
    gated_ref[0] = gated

    @pl.when(pl.program_id(0) == 0)
    def _():
        out_ref[...] = jnp.zeros_like(out_ref)

    out_ref[...] += dot(gated, output, 0, 0)


def mix_back_kernel(*refs):
    grad_ref, *sides = refs[:9]
    qa_ref, qb_ref, k_ref, r_ref, v_ref, o_ref, p_ref, every_ref, value_gate, output_gate = refs[9:19]
    dq_ref, dk_ref, dr_ref, dv_ref, dzv_ref, dzo_ref, du_ref, dw_ref, out_ref = refs[-9:]
    query, key, value, output = (lanes(*sides[i : i + 2]) for i in range(0, 8, 2))
    back = dot(output, grad_ref[...], 1, 1)
    gate = output_gate[0]
    dzo_ref[0] = expert_products(back, o_ref[0].astype(single)) * gate * (1.0 - gate)
    grad_out = sums_of_experts(gate, back).astype(bfloat)
    weights = p_ref[0]
    grad_mixed = dot(grad_out, weights.astype(bfloat), 1, 0).astype(bfloat).astype(single)
    grad = dot(grad_out, v_ref[0], 0, 0).astype(bfloat).astype(single)
    grad = weights * (grad - jnp.sum(grad * weights, axis=1, keepdims=True)) * scale
    low = grad.astype(bfloat)
    grad_qa = dot(k_ref[0], low, 1, 1).astype(bfloat).astype(single)
    grad_key = dot(qa_ref[0], low, 1, 0).astype(bfloat)
    row = lax.broadcasted_iota(jnp.int32, (SEG, SEG), 0)
    column = lax.broadcasted_iota(jnp.int32, (SEG, SEG), 1)
    turn = jnp.where(row + column == SEG - 1, 1.0, 0.0).astype(bfloat)
    far = pltpu.roll(dot(turn, low, 1, 0), 0, 1, stride=1, stride_axis=0).astype(bfloat)
    dr_ref[0] = dot(dot(qb_ref[0], turn, 1, 0).astype(bfloat), far, 1, 0).astype(bfloat)
    grad_qb = dot(dot(r_ref[0], far, 1, 1).astype(bfloat), turn, 1, 0)
    du_ref[0] = jnp.sum(grad_qa, axis=1, keepdims=True)
    dw_ref[0] = jnp.sum(grad_qb, axis=1, keepdims=True)
    grad_query = (grad_qa + grad_qb).astype(bfloat)
    dq_ref[0, :, :MEM] = jnp.zeros((DH, MEM), bfloat)
    dq_ref[0, :, MEM:] = grad_query
    dk_ref[0] = grad_key
    gate = value_gate[0]
    dzv_ref[0] = expert_products(every_ref[0], grad_mixed) * gate * (1.0 - gate)
    grad_value = each_expert(gate, grad_mixed)
    dv_ref[0] = grad_value

    @pl.when(pl.program_id(0) == 0)
    def _():
        out_ref[...] = jnp.zeros_like(out_ref)

    out_ref[...] += dot(grad_key, key, 0, 0) + dot(grad_value, value, 0, 0)
    out_ref[MEM:, :] += dot(grad_query, query, 0, 0)


def head_rows(rows, columns, dtype=bfloat):
    block = pl.BlockSpec((1, rows, columns), lambda h: (h, 0, 0))
    return block, jax.ShapeDtypeStruct((H, rows, columns), dtype)


def weight_blocks(sides, start, rows):
    blocks, _, width = sides[0].shape
    return [pl.BlockSpec((blocks, rows, width), lambda h: (0, start // rows + h, 0))] * 2


def fixed(rows, columns):
    return pl.BlockSpec((rows, columns), lambda *_: (0, 0))


EXPERT = NE * DH


def mix(normed, rel, sides, content, position, value_gates, output_gates):
    outs = [
        head_rows(DH, SEG),
        head_rows(DH, SEG),
        head_rows(DH, SPAN),
        head_rows(DH, SPAN),
        head_rows(DH, SPAN),
        head_rows(DH, SEG),
        head_rows(SEG, SPAN, single),
        head_rows(EXPERT, SPAN),
        head_rows(EXPERT, SEG),
        (fixed(SEG, D), jax.ShapeDtypeStruct((SEG, D), single)),
    ]
    return pl.pallas_call(
        mix_kernel,
        grid=(H,),
        in_specs=[fixed(SPAN, D), fixed(SPAN, D)]
        + weight_blocks(sides, QUERY_ROW, DH)
        + weight_blocks(sides, QUERY_ROW + HD, DH)
        + weight_blocks(sides, POSITION_ROW, DH)
        + weight_blocks(sides, VALUE_ROW, EXPERT)
        + weight_blocks(sides, OUTPUT_ROW, EXPERT)
        + [head_rows(DH, 1)[0]] * 2
        + [head_rows(8, SPAN)[0], head_rows(8, SEG)[0]],
        out_specs=[spec for spec, _ in outs],
        out_shape=[shape for _, shape in outs],
        compiler_params=params,
        cost_estimate=light,
    )(normed, rel, *(sides * 5), content, position, value_gates, output_gates)


def mix_back(grad, sides, stored, value_gates, output_gates, ties):
    outs = [
        head_rows(DH, SPAN),
        head_rows(DH, SPAN),
        head_rows(DH, SPAN),
        head_rows(EXPERT, SPAN),
        head_rows(8, SPAN, single),
        head_rows(8, SEG, single),
        head_rows(DH, 1, single),
        head_rows(DH, 1, single),
        (fixed(SPAN, D), jax.ShapeDtypeStruct((SPAN, D), single)),
    ]
    return pl.pallas_call(
        mix_back_kernel,
        grid=(H,),
        in_specs=[fixed(SEG, D)]
        + weight_blocks(sides, QUERY_ROW, DH)
        + weight_blocks(sides, QUERY_ROW + HD, DH)
        + weight_blocks(sides, VALUE_ROW, EXPERT)
        + weight_blocks(sides, OUTPUT_ROW, EXPERT)
        + [head_rows(*array.shape[1:])[0] for array in stored]
        + [head_rows(8, SPAN)[0], head_rows(8, SEG)[0]]
        + [untouched] * len(ties),
        out_specs=[spec for spec, _ in outs],
        out_shape=[shape for _, shape in outs],
        compiler_params=params,
        cost_estimate=light,
    )(grad, *(sides * 4), *stored, value_gates, output_gates, *ties)


ff_tile = 1024
ff_columns = pl.BlockSpec((SEG, ff_tile), lambda i: (0, i))
ff_weights = pl.BlockSpec((D // 2, ff_tile), lambda i: (0, i))
ff_bias = pl.BlockSpec((1, ff_tile), lambda i: (0, i))


def expand_kernel(in_ref, own_ref, other_ref, bias_ref, act_ref, slope_ref):
    hidden = dot(in_ref[:, : D // 2], own_ref[...], 1, 0) + bias_ref[...]
    hidden = hidden + dot(in_ref[:, D // 2 :], other_ref[...], 1, 0)
    share = 0.5 + 0.5 * lax.erf(hidden * math.sqrt(0.5))
    act_ref[...] = (hidden * share).astype(bfloat)
    density = jnp.exp(hidden * hidden * -0.5) * (1.0 / math.sqrt(2.0 * math.pi))
    slope_ref[...] = (share + hidden * density).astype(bfloat)


def expand_forward(normed, sides, bias):
    wide = jax.ShapeDtypeStruct((SEG, FF), bfloat)
    return pl.pallas_call(
        expand_kernel,
        grid=(FF // ff_tile,),
        in_specs=[fixed(SEG, D), ff_weights, ff_weights, ff_bias],
        out_specs=[ff_columns, ff_columns],
        out_shape=[wide, wide],
        compiler_params=params,
        cost_estimate=light,
    )(normed, *sides, bias)


def contract_kernel(act_ref, own_ref, other_ref, out_ref):
    @pl.when(pl.program_id(0) == 0)
    def _():
        out_ref[...] = jnp.zeros_like(out_ref)

    out_ref[:, : D // 2] += dot(act_ref[...], own_ref[...], 1, 1)
    out_ref[:, D // 2 :] += dot(act_ref[...], other_ref[...], 1, 1)


def contract_forward(active, sides):
    return pl.pallas_call(
        contract_kernel,
        grid=(FF // ff_tile,),
        in_specs=[ff_columns, ff_weights, ff_weights],
        out_specs=fixed(SEG, D),
        out_shape=jax.ShapeDtypeStruct((SEG, D), single),
        compiler_params=params,
        cost_estimate=light,
    )(active, *sides)


def ff_back_kernel(in_ref, slope_ref, own_down, other_down, own_up, other_up, *refs):
    grad_ref, bias_ref, out_ref, total = refs[-4:]
    tile = pl.program_id(0)

    @pl.when(tile == 0)
    def _():
        total[...] = jnp.zeros_like(total)

    grad = dot(in_ref[:, : D // 2], own_down[...], 1, 0)
    grad = grad + dot(in_ref[:, D // 2 :], other_down[...], 1, 0)
    grad = grad.astype(bfloat).astype(single) * slope_ref[...].astype(single)
    low = grad.astype(bfloat)
    grad_ref[...] = low
    bias_ref[...] = jnp.sum(low.astype(single), axis=0, keepdims=True)
    total[:, : D // 2] += dot(low, own_up[...], 1, 1)
    total[:, D // 2 :] += dot(low, other_up[...], 1, 1)

    @pl.when(tile == pl.num_programs(0) - 1)
    def _():
        out_ref[...] = total[...].astype(bfloat)


def ff_back(grad, slope, down, up, ties):
    return pl.pallas_call(
        ff_back_kernel,
        grid=(FF // ff_tile,),
        in_specs=[fixed(SEG, D), ff_columns] + [ff_weights] * 4 + [untouched] * len(ties),
        out_specs=[ff_columns, ff_bias, fixed(SEG, D)],
        out_shape=[
            jax.ShapeDtypeStruct((SEG, FF), bfloat),
            jax.ShapeDtypeStruct((1, FF), single),
            jax.ShapeDtypeStruct((SEG, D), bfloat),
        ],
        scratch_shapes=[pltpu.VMEM((SEG, D), single)],
        compiler_params=params,
        cost_estimate=light,
    )(grad, slope, *down, *up, *ties)


untouched = pl.BlockSpec(memory_space=pl.ANY)


def product_kernel(left_dim, adds, left_ref, right_ref, *refs):
    total = dot(left_ref[...], right_ref[...], left_dim, 0)
    if adds:
        total = total + refs[0][...].astype(single)
    refs[-1][...] = total.astype(bfloat)


def ff_product(wide, other, side, came=(), ties=()):
    return pl.pallas_call(
        functools.partial(product_kernel, 0, len(came)),
        grid=(FF // ff_tile,),
        in_specs=[pl.BlockSpec((SEG, D // 2), lambda i: (0, side)), ff_columns]
        + [ff_weights] * len(came)
        + [untouched] * len(ties),
        out_specs=ff_weights,
        out_shape=jax.ShapeDtypeStruct((D // 2, FF), bfloat),
        compiler_params=params,
        cost_estimate=light,
    )(wide, other, *came, *ties)


def expert_product(wide, other, side, came=(), ties=()):
    rows, depth = other.shape
    tile = pl.BlockSpec((EXPERT, D // 2), lambda i: (i, 0))
    return pl.pallas_call(
        functools.partial(product_kernel, 1, len(came)),
        grid=(rows // EXPERT,),
        in_specs=[
            pl.BlockSpec((EXPERT, depth), lambda i: (i, 0)),
            pl.BlockSpec((depth, D // 2), lambda i: (0, side)),
        ]
        + [tile] * len(came)
        + [untouched] * len(ties),
        out_specs=tile,
        out_shape=jax.ShapeDtypeStruct((rows, D // 2), bfloat),
        compiler_params=params,
        cost_estimate=light,
    )(other, wide, *came, *ties)


def table_product_kernel(first, adds, grad_ref, ids_ref, out_grad, in_grad, *refs):
    rows = grad_ref.shape[1]
    place = first + pl.program_id(0) * rows + lax.broadcasted_iota(jnp.int32, (rows, SEG), 0)
    chosen = jnp.where(place == ids_ref[...], 1.0, 0.0).astype(bfloat)
    total = dot(grad_ref[...], out_grad[...], 0, 0) + dot(chosen, in_grad[...], 1, 0)
    if adds:
        total = total + refs[0][...].astype(single)
    refs[-1][...] = total.astype(bfloat)


def table_product(grad_logits, ids, normed, grad_embedded, first, rows, side, came=(), ties=()):
    half = pl.BlockSpec((SEG, D // 2), lambda i: (0, side))
    tile = pl.BlockSpec((head_tile, D // 2), lambda i: (i, 0))
    return pl.pallas_call(
        functools.partial(table_product_kernel, first, len(came)),
        grid=(rows // head_tile,),
        in_specs=[
            pl.BlockSpec((SEG, head_tile), lambda i: (0, first // head_tile + i)),
            fixed(1, SEG),
            half,
            half,
        ]
        + [tile] * len(came)
        + [untouched] * len(ties),
        out_specs=tile,
        out_shape=jax.ShapeDtypeStruct((rows, D // 2), bfloat),
        compiler_params=params,
        cost_estimate=light,
    )(grad_logits, ids, normed, grad_embedded, *came, *ties)


def small_product_kernel(adds, q_ref, k_ref, r_ref, gates_ref, vectors_ref, normed, rel, *refs):
    out = refs[-1]

    def put(start, value):
        stop = start + value.shape[0]
        if adds:
            value = value + refs[0][start:stop, :].astype(single)
        out[start:stop, :] = value.astype(bfloat)

    put(0, dot(q_ref[...], normed[...], 1, 0))
    put(HD, dot(k_ref[...], normed[...], 1, 0))
    put(2 * HD, dot(r_ref[...], rel[...], 1, 0))
    put(3 * HD, dot(gates_ref[...], normed[...], 1, 0) + vectors_ref[...])


def small_product(grads, vectors, normed, rel, side, came=(), ties=()):
    def half(rows):
        return pl.BlockSpec((rows, D // 2), lambda i: (0, side))

    rows = 3 * HD + LAST_ROWS
    return pl.pallas_call(
        functools.partial(small_product_kernel, len(came)),
        grid=(1,),
        in_specs=[fixed(*grad.shape) for grad in grads]
        + [half(LAST_ROWS), half(SPAN), half(SPAN)]
        + [fixed(rows, D // 2)] * len(came)
        + [untouched] * len(ties),
        out_specs=fixed(rows, D // 2),
        out_shape=jax.ShapeDtypeStruct((rows, D // 2), bfloat),
        compiler_params=params,
        cost_estimate=light,
    )(*grads, vectors, normed, rel, *came, *ties)


def rows_kernel(own_ref, other_ref, out_ref):
    out_ref[...] = lanes(own_ref, other_ref)


def rows_of(sides, start, rows):
    blocks, _, width = sides[0].shape
    block = pl.BlockSpec((blocks, rows, width), lambda i: (0, start // rows, 0))
    return pl.pallas_call(
        rows_kernel,
        grid=(1,),
        in_specs=[block, block],
        out_specs=fixed(rows, D),
        out_shape=jax.ShapeDtypeStruct((rows, D), bfloat),
        compiler_params=params,
        cost_estimate=light,
    )(*sides)


def lookup_kernel(first, ids_ref, own_ref, other_ref, out_ref):
    tile = pl.program_id(0)
    rows = own_ref.shape[1]
    place = first + tile * rows + lax.broadcasted_iota(jnp.int32, (SEG, rows), 1)
    chosen = jnp.where(ids_ref[...] == place, 1.0, 0.0).astype(bfloat)
    found = dot(chosen, lanes(own_ref, other_ref), 1, 0)

    @pl.when(tile == 0)
    def _():
        out_ref[...] = found

    @pl.when(tile > 0)
    def _():
        out_ref[...] += found


def lookup(ids, own, other, first):
    blocks, rows, width = own.shape
    tile = 1024
    side = pl.BlockSpec((blocks, tile, width), lambda i: (0, i, 0))
    return pl.pallas_call(
        functools.partial(lookup_kernel, first),
        grid=(rows // tile,),
        in_specs=[pl.BlockSpec((SEG, 1), lambda i: (0, 0)), side, side],
        out_specs=pl.BlockSpec((SEG, D), lambda i: (0, 0)),
        out_shape=jax.ShapeDtypeStruct((SEG, D), single),
        compiler_params=params,
        cost_estimate=light,
    )(ids, own, other)


head_tile = 512


def head_kernel(
    shard_rows,
    shard_half,
    hf_ref,
    goal_ref,
    counted_ref,
    own_zero,
    other_zero,
    own_one,
    other_one,
    grad_ref,
    back_ref,
    loss_ref,
    logits,
    total,
    highest,
    summed,
    picked,
):
    tiles = pl.num_programs(0) // 2
    step = pl.program_id(0)
    tile = lax.rem(step, tiles)
    at = pl.multiple_of(tile * head_tile, head_tile)
    place = at + lax.broadcasted_iota(jnp.int32, (SEG, head_tile), 1)
    hits = place == goal_ref[...]

    def each_table(use):
        @pl.when(tile < tiles // 2)
        def _():
            use(lanes(own_zero, other_zero), 0)

        @pl.when(tile >= tiles // 2)
        def _():
            use(lanes(own_one, other_one), shard_half)

    def groups(values):
        return [values[:, i : i + 128] for i in range(0, head_tile, 128)]

    @pl.when(step == 0)
    def _():
        highest[...] = jnp.full_like(highest, masked)
        summed[...] = jnp.zeros_like(summed)
        picked[...] = jnp.zeros_like(picked)
        total[...] = jnp.zeros_like(total)

    @pl.when(step < tiles)
    def _():
        def use(rows, late):
            scores = dot(hf_ref[...], rows, 1, 1)
            scores = jnp.where(lax.rem(place, shard_half) + late < shard_rows, scores, masked)
            logits[:, pl.ds(at, head_tile)] = scores
            parts = groups(scores)
            top = functools.reduce(jnp.maximum, parts, highest[...])
            powers = sum(jnp.exp(part - top) for part in parts)
            summed[...] = summed[...] * jnp.exp(highest[...] - top) + powers
            highest[...] = top
            picked[...] += sum(groups(jnp.where(hits, scores, 0.0)))

        each_table(use)

    @pl.when(step == tiles)
    def _():
        top = jnp.max(highest[...], axis=1, keepdims=True)
        powers = jnp.sum(summed[...] * jnp.exp(highest[...] - top), axis=1, keepdims=True)
        whole = top + jnp.log(powers)
        loss_ref[...] = (whole - jnp.sum(picked[...], axis=1, keepdims=True)) * counted_ref[...]
        highest[...] = jnp.broadcast_to(whole, highest.shape)

    @pl.when(step >= tiles)
    def _():
        def use(rows, late):
            shares = jnp.exp(logits[:, pl.ds(at, head_tile)] - highest[:, :1])
            grad = ((shares - jnp.where(hits, 1.0, 0.0)) * counted_ref[...]).astype(bfloat)
            grad_ref[...] = grad
            total[...] += dot(grad, rows, 1, 0)

        each_table(use)

    @pl.when(step == 2 * tiles - 1)
    def _():
        back_ref[...] = total[...].astype(bfloat)


def head(hf, goals, counted, parts, shard_rows, shard_half):
    blocks, rows, width = parts[0][0].shape
    half_tiles = rows // head_tile
    tiles = 2 * half_tiles

    def side(part):
        def index(i):
            return 0, jnp.clip(lax.rem(i, tiles) - part * half_tiles, 0, half_tiles - 1), 0

        return pl.BlockSpec((blocks, head_tile, width), index)

    column = pl.BlockSpec((SEG, 1), lambda i: (0, 0))
    whole = pl.BlockSpec((SEG, D), lambda i: (0, 0))
    return pl.pallas_call(
        functools.partial(head_kernel, shard_rows, shard_half),
        grid=(2 * tiles,),
        in_specs=[whole, column, column, side(0), side(0), side(1), side(1)],
        out_specs=[
            pl.BlockSpec((SEG, head_tile), lambda i: (0, jnp.maximum(i - tiles, 0))),
            whole,
            column,
        ],
        out_shape=[
            jax.ShapeDtypeStruct((SEG, 2 * rows), bfloat),
            jax.ShapeDtypeStruct((SEG, D), bfloat),
            jax.ShapeDtypeStruct((SEG, 1), single),
        ],
        scratch_shapes=[
            pltpu.VMEM((SEG, 2 * rows), single),
            pltpu.VMEM((SEG, D), single),
            pltpu.VMEM((SEG, 128), single),
            pltpu.VMEM((SEG, 128), single),
            pltpu.VMEM((SEG, 128), single),
        ],
        compiler_params=params,
        cost_estimate=light,
    )(hf, goals, counted, *parts[0], *parts[1])


def chosen_experts(routes, slots, capacity):
    experts = jnp.arange(NE, dtype=jnp.int32)[None, :, None, None]
    turned = jnp.transpose(routes, (1, 2, 0))[:, None]
    kept = jnp.transpose(slots, (1, 2, 0))[:, None] < capacity
    return jnp.sum(((turned == experts) & kept).astype(single), axis=2)


def advance(weight, velocity, average, grad, factor, step_rate):
    clipped = grad * factor
    velocity_next = momentum_decay * velocity + clipped
    updated = weight - step_rate * (clipped + momentum_decay * velocity_next)
    return (velocity_next, updated, average + (updated - average) / (STEP + 1))


def table_shape(grid):
    rows = V // grid.n_fsdp
    return rows, -(-rows // 256) * 128


def table_place(grid, ids):
    rows, part = table_shape(grid)
    owner, row = ids // rows, ids % rows
    return (row // part) * (grid.n_fsdp * part) + owner * part + row % part


def body(
    token_ids,
    targets,
    target_counts,
    memory,
    value_routes,
    value_slots,
    output_routes,
    output_slots,
    *states,
):
    masters, moments, averages = states[0::3], states[1::3], states[2::3]
    embedding, projector, position, values, outputs, expand, contract, vectors, biases = masters
    grid = Grid()
    ids = table_place(grid, token_ids[0])
    goals = table_place(grid, targets[0])
    half = D // 2
    chunk = D // grid.count

    shard_rows, shard_half = table_shape(grid)
    part_rows = shard_half * grid.n_fsdp
    table_shard = jnp.pad(embedding.astype(bfloat), ((0, 2 * shard_half - shard_rows), (0, 0)))
    expanding = Gather(grid, expand.astype(bfloat))
    contracting = Gather(grid, contract.T.astype(bfloat))
    tables = [Gather(grid, table_shard[i : i + shard_half]) for i in (0, shard_half)]
    attention_shard = jnp.concatenate(
        [
            values.astype(bfloat),
            outputs.T.astype(bfloat),
            projector[:, :QUERIES].astype(bfloat),
            position.astype(bfloat),
            projector[:, QUERIES:].astype(bfloat),
            vectors.T.astype(bfloat),
            jnp.zeros((chunk, LAST_ROWS - GATES - 4), bfloat),
        ],
        axis=1,
    )
    attending = Gather(grid, attention_shard, True)
    distances = jnp.array(grid.relative_blocks(), jnp.int32)
    width = D // grid.n_dp
    true_columns = (
        (distances[:, None] ^ grid.dp_index) * width + jnp.arange(width, dtype=jnp.int32)[None, :]
    ).reshape(D)
    to_order = (jnp.arange(D, dtype=jnp.int32)[:, None] == true_columns[None, :]).astype(bfloat)
    memory_rows = dot(memory[0], to_order, 1, 0)
    rel_table = dot(positions(SPAN, D).astype(bfloat), to_order, 1, 0).astype(bfloat)

    tables[0].direct_line()
    grid.step(memory_rows, rel_table)
    tables[0].neighbours()
    tables[1].direct_line()
    grid.step()
    attending.direct_line()
    opposite_and_neighbours(tables[0], tables[1])
    middle = expand.shape[1]
    lines = lax.all_gather(
        after(jnp.concatenate([expanding.shard, contracting.shard], axis=1), *grid.before),
        FSDP,
        axis=0,
        tiled=True,
    )
    expanding.line, contracting.line = lines[:, :middle], lines[:, middle:]
    tables[1].opposite()
    tables[0].pair()
    attending.neighbours()
    grid.step()
    attending.opposite()
    expanding.neighbours()
    tables[1].pair()
    found = [lookup(ids[:, None], *tables[0].by_block(), 0)]
    grid.step(found[0])
    tables_by_block = [part.by_block() for part in tables]
    attending.pair()
    expanding.opposite()
    found.append(lookup(ids[:, None], *tables_by_block[1], part_rows))
    embedded = (found[0] + found[1]) * D**0.5
    grid.step(embedded)
    contracting.neighbours()
    expanding.pair()
    attention = attending.by_block()
    last_rows = rows_of(attention, GATE_ROW, LAST_ROWS)
    gains = last_rows[GATES : GATES + 4].astype(single)

    stream = jnp.concatenate([memory_rows, embedded], axis=0)
    normal_in, spread_in = normalised(stream)
    normed = (normal_in * gains[0]).astype(bfloat)
    logits = jax.nn.sigmoid(dot(last_rows, normed, 1, 1)[:GATES])

    def gates_of(shares, routes, slots, capacity):
        kept = shares.reshape(H, NE, -1) * chosen_experts(routes, slots, capacity)
        return jnp.pad(kept, ((0, 0), (0, 8 - NE), (0, 0)))

    value_gates = gates_of(logits[: H * NE], value_routes[0], value_slots[0], CAPV)
    output_gates = gates_of(logits[H * NE :, MEM:], output_routes[0], output_slots[0], CAPO)
    *stored, gated, mixed = mix(
        normed,
        rel_table,
        attention,
        biases[:HD].reshape(H, DH, 1),
        biases[HD : 2 * HD].reshape(H, DH, 1),
        value_gates,
        output_gates,
    )
    grid.step(mixed)
    contracting.opposite()
    gated = gated.reshape(H * EXPERT, SEG)
    residual = embedded + mixed
    normal_mid, spread_mid = normalised(residual)
    normed_mid = (normal_mid * gains[1]).astype(bfloat)
    up = expanding.sides()
    active, slope = expand_forward(normed_mid, up, biases[None, 2 * HD :])
    grid.step()
    contracting.pair()
    grid.step()
    down = contracting.sides()
    final = residual + contract_forward(active, down) + gains[3]
    normal_out, spread_out = normalised(final)
    normed_out = (normal_out * gains[2]).astype(bfloat)

    counted = (jnp.arange(SEG, dtype=jnp.int32) < target_counts[0]).astype(single)
    grad_logits, grad_out, losses = head(
        normed_out, goals[:, None], counted[:, None], tables_by_block, shard_rows, shard_half
    )
    loss = jnp.sum(losses)

    grad_final, grad_gain_out = norm_gradient(
        grad_out.astype(single), normal_out, spread_out, gains[2]
    )
    grad_branch = grad_final.astype(bfloat)
    grad_bias_down = jnp.sum(grad_branch.astype(single), axis=0)

    def summing(wide, other):
        return Reduce(grid, functools.partial(ff_product, wide, other))

    def summing_turned(wide, other):
        return Reduce(grid, functools.partial(expert_product, wide, other), True, True)

    grid.step()
    contracting = summing(grad_branch, active)
    contracting.pair()
    grad_hidden, grad_bias_up, grad_mid = ff_back(
        grad_branch, slope, down, up, [contracting.high]
    )
    expanding = summing(normed_mid, grad_hidden)
    expanding.pair()
    contracting.opposite(expanding.high)
    expanding.opposite(contracting.total)
    grad_residual, grad_gain_mid = norm_gradient(
        grad_mid.astype(single), normal_mid, spread_mid, gains[1]
    )
    grad_residual = grad_residual + grad_final
    low_residual = grad_residual.astype(bfloat)
    outputting = summing_turned(low_residual, gated)
    outputting.pair(expanding.total)
    contracting.neighbours()
    expanding.neighbours()
    (
        grad_queries,
        grad_keys,
        grad_rel,
        grad_values,
        grad_value_gates,
        grad_output_gates,
        grad_content,
        grad_position,
        grad_normed,
    ) = mix_back(
        low_residual,
        attention,
        stored,
        value_gates,
        output_gates,
        [outputting.high, *contracting.away, *expanding.away],
    )
    grad_values = grad_values.reshape(H * EXPERT, SPAN)
    valuing = summing_turned(normed, grad_values)
    valuing.pair(*contracting.sums)
    outputting.opposite(valuing.high)
    grad_gates = jnp.concatenate(
        [
            grad_value_gates[:, :NE].reshape(H * NE, SPAN),
            jnp.pad(grad_output_gates[:, :NE].reshape(H * NE, SEG), ((0, 0), (MEM, 0))),
            jnp.zeros((LAST_ROWS - GATES, SPAN), single),
        ],
        axis=0,
    ).astype(bfloat)
    contracting.along_line()
    grad_normed = (grad_normed + dot(grad_gates, last_rows, 0, 0)).astype(bfloat)
    grad_stream, grad_gain_in = norm_gradient(
        grad_normed.astype(single), normal_in, spread_in, gains[0]
    )
    grad_embedded = (grad_residual + grad_stream[MEM:]).astype(bfloat)
    grad_vectors = jnp.pad(
        jnp.stack([grad_gain_in, grad_gain_mid, grad_gain_out, grad_bias_down]),
        ((GATES, LAST_ROWS - GATES - 4), (0, 0)),
    )

    def table_summing(first):
        part = functools.partial(
            table_product,
            grad_logits,
            ids[None, :],
            normed_out,
            grad_embedded * bfloat(D**0.5),
            first,
            part_rows,
        )
        return Reduce(grid, part, True)

    tables = [table_summing(i) for i in (0, part_rows)]
    grads = [part.reshape(HD, SPAN) for part in (grad_queries, grad_keys, grad_rel)] + [grad_gates]
    small = functools.partial(small_product, grads, grad_vectors, normed, rel_table)
    smalling = Reduce(grid, small, True, True)
    expanding.along_line()
    outputting.neighbours()
    tables[0].pair(outputting.total, *expanding.sums)
    smalling.pair(tables[0].high)
    valuing.opposite(smalling.high, *outputting.met)
    outputting.along_line()
    tables[1].pair(valuing.total, contracting.shard)
    smalling.opposite(tables[1].high)
    valuing.neighbours()
    tables[0].opposite(smalling.total, *valuing.met, *outputting.sums)
    smalling.neighbours()
    tables[1].opposite(tables[0].total, *valuing.sums, *smalling.met)
    tables[0].neighbours()
    tables[1].neighbours()
    for part in (valuing, smalling, tables[0], tables[1]):
        part.along_line()
    sum_contract, sum_expand, sum_outputs, sum_values, sum_small = (
        part.value() for part in (contracting, expanding, outputting, valuing, smalling)
    )
    sum_table = jnp.concatenate([part.value() for part in tables], axis=0)[:shard_rows]

    shard_grads = [
        sum_table,
        jnp.concatenate([sum_small[:, :QUERIES], sum_small[:, 3 * HD : 3 * HD + GATES]], axis=1),
        sum_small[:, QUERIES : 3 * HD],
        sum_values,
        sum_outputs.T,
        sum_expand,
        sum_contract.T,
        sum_small[:, 3 * HD + GATES : 3 * HD + GATES + 4].T,
    ]
    most_tokens = grid.count * SEG
    local_squares = jnp.zeros((), single)
    for part in tables + [contracting, expanding, outputting, valuing, smalling]:
        scaled = part.value() * (1.0 / most_tokens)
        local_squares = local_squares + jnp.sum(scaled * scaled)
    shared = jnp.concatenate(
        [
            grad_content.reshape(HD),
            grad_position.reshape(HD),
            grad_bias_up.reshape(FF),
            jnp.stack([loss, target_counts[0].astype(single), local_squares]),
        ]
    )
    shared = total_everywhere(grid, shared)
    bias_grad, loss_total, token_count, squares = shared[:-3], shared[-3], shared[-2], shared[-1]
    scaled = bias_grad * (1.0 / most_tokens)
    gradient_norm = jnp.sqrt(squares + jnp.sum(scaled * scaled)) * (most_tokens / token_count)
    factor = jnp.minimum(1.0, clip_norm / (gradient_norm + 1e-06))
    inverse = 1.0 / token_count
    shard_grads = [grad * inverse for grad in shard_grads]
    bias_grad = bias_grad * inverse
    step_rate = rate_base * (PARAMS / D) ** 0.5
    results = (loss_total, token_count, gradient_norm)
    for weight, velocity, average, grad, multiplier in zip(
        masters, moments, averages, shard_grads + [bias_grad], rate_factors
    ):
        results += advance(weight, velocity, average, grad, factor, step_rate * multiplier)
    return results


def solution(mesh):
    batch = P(BOTH)
    rows, columns, whole = P(BOTH, None), P(None, BOTH), P()
    kinds = (P(FSDP, DP), rows, rows, rows, columns, rows, columns, columns, whole)
    triples = tuple(kind for kind in kinds for _ in range(3))
    return jax.shard_map(
        body,
        mesh=mesh,
        in_specs=(batch,) * 8 + triples,
        out_specs=(whole,) * 3 + triples,
        check_vma=False,
    )
```
